256 devices in a mesh: slab: 64 (over x, z, core), spd: 4 (over y).
Axes of the slice: x: 4, y: 4, z: 8, core: 2. Of those that a mesh axis runs over, the one named last changes fastest.
Arguments:
- mode_shapes: bfloat16 [131072, 512], P('slab'), may hold values from -6 to 6
- unbalance: bfloat16 [2, 131072], P(None, 'slab'), may hold values from -1 to 1
- connectivity: int32 [8, 131072], P(None, 'slab'), may hold values from 0 to 3071, as said below
- stress_weights: bfloat16 [8, 131072], P(None, 'slab'), may hold values from -0.01171875 to 0.01171875
- face_low_nodes: int32 [32768], P('slab'), may hold values from 0 to 2047
- face_high_nodes: int32 [32768], P('slab'), may hold values from 0 to 2047
- natural_freq: float32 [256], replicated, may hold values from 0.5 to 4
- damping_ratio: float32 [256], replicated, may hold values from 0.003 to 0.02
- coupling: float32 [256, 256], replicated, may hold values from -1 to 1
- speed_index: int32 [1024], P('spd'), may hold values from 0 to 4095
Outputs:
- stress_peak: float32 [131072], P('slab')
The draws below stay inside these ranges and needn't reach their ends.
Inputs may be any that keep to these rules, and one draw needn't show every extreme that they name: For an element e with i = e mod 2048, connectivity[k, e] - i lies in 0 to 1024, and the 8 nodes of an element are distinct.
All inputs are finite; a program needn't handle non-finite values.
Results may differ from the reference program's by a relative error of at most 0.0027.
Values may be sent and summed in bfloat16 or wider, within the bound.
No kernel may reach another device: no remote copies, remote signals or barrier semaphores. Data moves between devices by JAX's collectives and lax.ppermute only.
A program may use at most 64 MiB of HBM per device.

```python
import math
import jax
import jax.numpy as jnp
from jax import lax

M = 256
R = 2048
H = 512
K = 8
ITERS = 6
NGRID = 4096
DOF = 131072
ELEMS = 131072
SPEEDS = 1024
N_SLAB = 64


def draw_unbalance(key, part):
    key = jax.random.fold_in(key, 11)
    position = jnp.arange(DOF, dtype=jnp.float32) / DOF
    ramp = (1.0 + 2.0 * position) / math.sqrt(DOF)
    base = jnp.clip(jax.random.normal(key, (2, DOF), jnp.float32), -3.0, 3.0)
    return (base * ramp[None, :]).astype(jnp.bfloat16)


def draw_connectivity(key, part):
    key = jax.random.fold_in(key, 23)
    bucket = (2 * H + 1) // K
    lowest = jnp.arange(K, dtype=jnp.int32) * (2 * H + 1) // K
    extra = jax.random.randint(key, (K, ELEMS), 0, bucket, jnp.int32)
    local = jnp.arange(ELEMS, dtype=jnp.int32) % R
    corner = jnp.arange(K, dtype=jnp.int32)
    first_spot = (corner[:, None] == 0) & (local[None, :] == 0)
    last_spot = (corner[:, None] == K - 1) & (local[None, :] == R - 1)
    extra = jnp.where(first_spot, 0, extra)
    extra = jnp.where(last_spot, 2 * H - lowest[:, None], extra)
    return local[None, :] + lowest[:, None] + extra


def set_ends(array, rng, smallest, top_value):
    dims = array.shape
    spot = [jax.random.randint(jax.random.fold_in(rng, axis), (), 0, dims[axis]) for axis in range(len(dims))]
    array = array.at[tuple(spot)].set(smallest)
    longest = dims.index(max(dims))
    spot[longest] = (spot[longest] + 1) % dims[longest]
    return array.at[tuple(spot)].set(top_value)


def steps_of(rng, dims, split, least, largest):
    factor_of = 1.0
    for dim, parts in split:
        heights = jax.random.uniform(jax.random.fold_in(jax.random.fold_in(rng, 6), dim), (parts,), jnp.float32, least / len(split), largest / len(split))
        factor_of = factor_of * jnp.repeat(jnp.exp(heights), dims[dim] // parts).reshape((-1,) + (1,) * (len(dims) - 1 - dim))
    return factor_of


def scatter_about(key, dims, spread, most, pieces=(), held_as=jnp.bfloat16):
    entries = jax.random.normal(key, dims, jnp.float32) * spread
    if len(pieces) > 0:
        entries = steps_of(key, dims, pieces, -0.22, 0.18) * entries
    return jnp.clip(entries, min=-most, max=most).astype(held_as)


def setup_inputs(seed: int = 0) -> dict:
    splits = jax.random.split(jax.random.key(seed), 11)
    return {
        "mode_shapes": scatter_about(splits[0], (DOF, 2 * M), 1.0, 6.0, ((0, 64),)),
        "unbalance": draw_unbalance(jax.random.fold_in(splits[10], 71), 0),
        "connectivity": draw_connectivity(jax.random.fold_in(splits[10], 71), 0),
        "stress_weights": scatter_about(splits[3], (K, ELEMS), (64 * K * 2 * M) ** -0.5, 0.01171875, ((1, 64),)),
        "face_low_nodes": set_ends(jax.random.randint(splits[4], (H * N_SLAB,), 0, R), jax.random.fold_in(splits[4], 1), 0, R - 1).astype(jnp.int32),
        "face_high_nodes": set_ends(jax.random.randint(splits[5], (H * N_SLAB,), 0, R), jax.random.fold_in(splits[5], 1), 0, R - 1).astype(jnp.int32),
        "natural_freq": jnp.clip(jnp.exp(jax.random.uniform(splits[6], (M,), jnp.float32, math.log(0.5), math.log(4.0))), 0.5, 4.0),
        "damping_ratio": jnp.clip(jnp.exp(jax.random.uniform(splits[7], (M,), jnp.float32, math.log(0.003), math.log(0.02))), 0.003, 0.02),
        "coupling": jnp.clip(jax.random.uniform(splits[8], (M, M), jnp.float32, -1.0, 1.0), -1.0, 1.0),
        "speed_index": set_ends(jax.random.randint(splits[9], (SPEEDS,), 0, NGRID), jax.random.fold_in(splits[9], 1), 0, NGRID - 1).astype(jnp.int32),
    }


def modal_solve(force_re, force_im, omega, natural_freq, damping_ratio, coupling):
    count = natural_freq.shape[0]
    off_diagonal = 1.0 - jnp.eye(count, dtype=jnp.float32)
    row_scale = damping_ratio * natural_freq * (1.5 / math.sqrt(count))
    coupled = coupling * row_scale[:, None] * off_diagonal
    omega_sq = omega * omega
    denom_re = (natural_freq * natural_freq)[:, None] - omega_sq[None, :]
    denom_im = 2.0 * (damping_ratio * natural_freq)[:, None] * omega[None, :]
    inverse = 1.0 / (denom_re * denom_re + denom_im * denom_im)
    load_re = force_re[:, None] * omega_sq[None, :]
    load_im = force_im[:, None] * omega_sq[None, :]

    def divide(top_re, top_im):
        return ((top_re * denom_re + top_im * denom_im) * inverse, (top_im * denom_re - top_re * denom_im) * inverse)
    coord_re, coord_im = divide(load_re, load_im)
    for sweep in range(ITERS):
        product_re = jnp.dot(coupled, coord_re, precision=lax.Precision.HIGHEST)
        product_im = jnp.dot(coupled, coord_im, precision=lax.Precision.HIGHEST)
        coord_re, coord_im = divide(load_re + omega[None, :] * product_im, load_im - omega[None, :] * product_re)
    return (coord_re, coord_im)

def peak_of(stress_modes, coord_re, coord_im):
    columns = jnp.concatenate([jnp.concatenate([coord_re, -coord_im], 0), jnp.concatenate([coord_im, coord_re], 0)], 1)
    stress = jnp.dot(stress_modes, columns, preferred_element_type=jnp.float32)
    speed_count = coord_re.shape[1]
    magnitude = jnp.sqrt(stress[:, :speed_count] ** 2 + stress[:, speed_count:] ** 2)
    return lax.optimization_barrier(jnp.max(magnitude, axis=1))

def reference(mode_shapes, unbalance, connectivity, stress_weights, face_low_nodes, face_high_nodes, natural_freq, damping_ratio, coupling, speed_index):
    product = jnp.dot(unbalance, mode_shapes, preferred_element_type=jnp.float32)
    force_re = product[0, :M] - product[1, M:]
    force_im = product[0, M:] + product[1, :M]
    omega = 0.25 + 4.0 * speed_index.astype(jnp.float32) / NGRID
    coord_re, coord_im = modal_solve(force_re, force_im, omega, natural_freq, damping_ratio, coupling)
    coord_re = coord_re.astype(jnp.bfloat16)
    coord_im = coord_im.astype(jnp.bfloat16)
    shapes_by_slab = mode_shapes.reshape(N_SLAB, R, 2 * M)
    low_nodes = face_low_nodes.reshape(N_SLAB, H)
    high_nodes = face_high_nodes.reshape(N_SLAB, H)
    links = connectivity.reshape(K, N_SLAB, R).transpose(1, 0, 2)
    recovery = stress_weights.reshape(K, N_SLAB, R).transpose(1, 0, 2)

    def one_slab(slab_number):
        own = shapes_by_slab[slab_number]
        below = jnp.maximum(slab_number - 1, 0)
        above = jnp.minimum(slab_number + 1, N_SLAB - 1)
        from_below = shapes_by_slab[below][high_nodes[below]]
        from_below = jnp.where(slab_number > 0, from_below, jnp.zeros_like(from_below))
        from_above = shapes_by_slab[above][low_nodes[above]]
        from_above = jnp.where(slab_number < N_SLAB - 1, from_above, jnp.zeros_like(from_above))
        extended = jnp.concatenate([from_below, own, from_above], 0)
        slab_links = links[slab_number]
        slab_weights = recovery[slab_number].astype(jnp.float32)
        accumulated = jnp.zeros((R, 2 * M), jnp.float32)
        for corner in range(K):
            accumulated = accumulated + slab_weights[corner][:, None] * extended[slab_links[corner]].astype(jnp.float32)
        stress_modes = accumulated.astype(jnp.bfloat16)
        return peak_of(stress_modes, coord_re, coord_im)
    peaks = lax.map(one_slab, jnp.arange(N_SLAB, dtype=jnp.int32))
    return peaks.reshape(N_SLAB * R)
```

```python
import functools
import math

import jax
import jax.numpy as jnp
from jax import lax
from jax.experimental import pallas as pl
from jax.experimental.pallas import tpu as pltpu
from jax.sharding import PartitionSpec as P

ITERS = 6
NGRID = 4096
X, Z, CORES = 4, 8, 2
BLOCK = 256
WINDOW = 1280
GROUP = 16
NN = (((1,), (0,)), ((), ()))
NT = (((1,), (1,)), ((), ()))


def mm(a, b, dims=NN):
    return lax.dot_general(a, b, dims, preferred_element_type=jnp.float32)


def vmem_call(body, out_shape, operands, scratch=(), flops=0, moved=0):
    spec = pl.BlockSpec(memory_space=pltpu.VMEM)
    many = isinstance(out_shape, (list, tuple))
    return pl.pallas_call(
        body,
        out_shape=out_shape,
        in_specs=[spec] * len(operands),
        out_specs=[spec] * len(out_shape) if many else spec,
        scratch_shapes=list(scratch),
        compiler_params=pltpu.CompilerParams(vmem_limit_bytes=24 << 20),
        cost_estimate=pl.CostEstimate(flops=flops, bytes_accessed=moved, transcendentals=0),
    )(*operands)


def slab_pairs(partner):
    pairs = []
    for x in range(X):
        for z in range(Z):
            for c in range(CORES):
                px, pz, pc = partner(x, z, c)
                pairs.append(((x * Z + z) * CORES + c, (px * Z + pz) * CORES + pc))
    return pairs


ROUNDS = (
    slab_pairs(lambda x, z, c: (x, z, 1 - c)),
    slab_pairs(lambda x, z, c: (x ^ 1, z, c)),
    slab_pairs(lambda x, z, c: (3 - x, z, c)),
    slab_pairs(lambda x, z, c: (x, z ^ 1, c)),
    slab_pairs(lambda x, z, c: (x, z ^ 2, c)),
    slab_pairs(lambda x, z, c: (x, 7 - z, c)),
)


def sum_over_slabs(x):
    for pairs in ROUNDS:
        x = x + lax.ppermute(x, "slab", pairs)
    return x


def from_behind(x, axis, by):
    count = lax.axis_size(axis)
    pairs = [(i, i + by) for i in range(count) if 0 <= i + by < count]
    return lax.ppermute(x, axis, pairs)


def gather_body(nodes, shapes, out, table):
    count, rows = table.shape
    place = jnp.transpose(jnp.broadcast_to(nodes[...], (8, count)))
    column = lax.broadcasted_iota(jnp.int16, (GROUP, rows), 1)
    for r in range(0, count, GROUP):
        here = jnp.broadcast_to(place[r : r + GROUP, 0:1], (GROUP, 128)).astype(jnp.int16)
        here = jnp.concatenate([here] * (rows // 128), 1)
        table[r : r + GROUP, :] = jnp.where(
            here == column, jnp.ones((), jnp.bfloat16), jnp.zeros((), jnp.bfloat16)
        )
    out[...] = mm(table[...], shapes[...]).astype(jnp.bfloat16)


def gather_rows(nodes, shapes):
    count, (rows, width) = nodes.shape[0], shapes.shape
    return vmem_call(
        gather_body,
        jax.ShapeDtypeStruct((count, width), shapes.dtype),
        (nodes.reshape(1, count), shapes),
        [pltpu.VMEM((count, rows), jnp.bfloat16)],
        flops=2 * count * rows * width,
    )


def fill_table(table, links, weights, start):
    place = jnp.transpose(links) - start
    weight = jnp.transpose(weights.astype(jnp.float32))
    corners = links.shape[0]
    column = lax.broadcasted_iota(jnp.int16, (GROUP, WINDOW), 1)
    for r in range(0, BLOCK, GROUP):
        row = jnp.zeros((GROUP, WINDOW), jnp.bfloat16)
        for k in range(corners):
            here = jnp.broadcast_to(place[r : r + GROUP, k : k + 1], (GROUP, 128)).astype(jnp.int16)
            value = jnp.broadcast_to(weight[r : r + GROUP, k : k + 1], (GROUP, 128)).astype(jnp.bfloat16)
            here = jnp.concatenate([here] * (WINDOW // 128), 1)
            value = jnp.concatenate([value] * (WINDOW // 128), 1)
            row = jnp.where(here == column, value, row)
        table[r : r + GROUP, :] = row


def middle_body(links, weights, shapes, out, tables):
    for b in range(2, 6):
        s = pl.ds(b * BLOCK, BLOCK)
        fill_table(tables.at[b % 2], links[:, s], weights[:, s], b * BLOCK)
        first = (b - 2) * BLOCK
        out[pl.ds(first, BLOCK), :] = mm(tables[b % 2], shapes[first : first + WINDOW, :]).astype(jnp.bfloat16)


def low_body(links, weights, below, shapes, out, tables):
    for b in range(2):
        s = pl.ds(b * BLOCK, BLOCK)
        fill_table(tables.at[b], links[:, s], weights[:, s], b * BLOCK)
        halo = (2 - b) * BLOCK
        total = mm(tables[b, :, :halo], below[b * BLOCK :, :])
        total += mm(tables[b, :, halo:], shapes[: WINDOW - halo, :])
        out[s, :] = total.astype(jnp.bfloat16)


def high_body(links, weights, shapes, above, out, tables):
    rows = shapes.shape[0]
    for b in range(2):
        s = pl.ds((6 + b) * BLOCK, BLOCK)
        fill_table(tables.at[b], links[:, s], weights[:, s], (6 + b) * BLOCK)
        halo = (1 + b) * BLOCK
        own = WINDOW - halo
        total = mm(tables[b, :, :own], shapes[rows - own :, :])
        total += mm(tables[b, :, own:], above[:halo, :])
        out[pl.ds(b * BLOCK, BLOCK), :] = total.astype(jnp.bfloat16)


def stress_modes_of(links, weights, below, shapes, above):
    width = shapes.shape[1]
    tables = [pltpu.VMEM((2, BLOCK, WINDOW), jnp.bfloat16)]

    def call(body, blocks, operands):
        return vmem_call(
            body,
            jax.ShapeDtypeStruct((blocks * BLOCK, width), jnp.bfloat16),
            operands,
            tables,
            flops=4 * blocks * BLOCK * WINDOW * width,
        )

    middle = call(middle_body, 4, (links, weights, shapes))
    low = call(low_body, 2, (links, weights, below, shapes))
    high = call(high_body, 2, (links, weights, shapes, above))
    return low, middle, high


def split(x):
    high = x.astype(jnp.bfloat16)
    return high, (x - high.astype(jnp.float32)).astype(jnp.bfloat16)


def prepare_body(speeds, freq, damping, coupling, u_re, u_im, omega_out, c_high, c_low):
    count = freq.shape[1]
    total = speeds.shape[1]
    omega = 0.25 + 4.0 * speeds[...].astype(jnp.float32) / NGRID
    omega = jnp.transpose(jnp.broadcast_to(omega, (8, total)))[:, 0:1]
    omega = jnp.broadcast_to(omega, (total, count))
    f = freq[...]
    zeta = damping[...]
    d_re = f * f - omega * omega
    d_im = 2.0 * (zeta * f) * omega
    scale = omega / (d_re * d_re + d_im * d_im)
    u_re[...] = d_re * scale
    u_im[...] = d_im * scale
    omega_out[...] = omega[:, :128]
    i = lax.broadcasted_iota(jnp.int32, (count, count), 0)
    j = lax.broadcasted_iota(jnp.int32, (count, count), 1)
    coupled = jnp.transpose(coupling[...]) * (zeta * f * (1.5 / math.sqrt(count)))
    c_high[...], c_low[...] = split(jnp.where(i == j, 0.0, coupled))


def prepare(speeds, freq, damping, coupling):
    total, count = speeds.shape[0], freq.shape[0]
    sds = jax.ShapeDtypeStruct
    return vmem_call(
        prepare_body,
        [
            sds((total, count), jnp.float32),
            sds((total, count), jnp.float32),
            sds((total, 128), jnp.float32),
            sds((count, count), jnp.bfloat16),
            sds((count, count), jnp.bfloat16),
        ],
        (speeds.reshape(1, total), freq.reshape(1, count), damping.reshape(1, count), coupling),
        flops=1 << 30,
    )


def solve_into(force, u_re, u_im, omega, c_high, c_low, store):
    f_re, f_im = force[0:1, :], force[1:2, :]
    ch, cl = c_high[...], c_low[...]

    def coupled(y):
        high, low = split(y)
        return mm(high, ch) + (mm(low, ch) + mm(high, cl))

    total, count = u_re.shape
    tile = 256
    tiles = [pl.ds(t, tile) for t in range(0, total, tile)]
    state = []
    for s in tiles:
        ur, ui = u_re[s, :], u_im[s, :]
        state.append((f_re * ur + f_im * ui, f_im * ur - f_re * ui))
    for sweep in range(ITERS):
        after = []
        for s, (yr, yi) in zip(tiles, state):
            pr, pi = coupled(yr), coupled(yi)
            ur, ui = u_re[s, :], u_im[s, :]
            top_re, top_im = f_re + pi, f_im - pr
            after.append((top_re * ur + top_im * ui, top_im * ur - top_re * ui))
        state = after
    for s, (yr, yi) in zip(tiles, state):
        w = omega[s, :]
        w = jnp.concatenate([w] * (count // 128), 1)
        store(s, (yr * w).astype(jnp.bfloat16), (yi * w).astype(jnp.bfloat16))


def peaks_body(force, u_re, u_im, omega, c_high, c_low, low, middle, high, out, for_re, for_im):
    count = u_re.shape[1]
    total = u_re.shape[0]

    def store(s, re, im):
        for_re[s, :count] = re
        for_re[s, count:] = -im
        for_im[s, :count] = im
        for_im[s, count:] = re

    solve_into(force, u_re, u_im, omega, c_high, c_low, store)
    tile = 256
    at = 0
    for part in (low, middle, high):
        for e in range(0, part.shape[0], BLOCK):
            modes = part[e : e + BLOCK, :]
            best = jnp.zeros((8, BLOCK), jnp.float32)
            for s in range(0, total, tile):
                re = mm(for_re[s : s + tile, :], modes, NT)
                im = mm(for_im[s : s + tile, :], modes, NT)
                square = re * re + im * im
                best = jnp.maximum(best, jnp.max(square.reshape(tile // 8, 8, BLOCK), axis=0))
            out[0:1, at : at + BLOCK] = jnp.sqrt(jnp.max(best, axis=0, keepdims=True))
            at += BLOCK


def peaks(force, prepared, parts):
    total, count = prepared[0].shape
    rows = sum(p.shape[0] for p in parts)
    out = vmem_call(
        peaks_body,
        jax.ShapeDtypeStruct((1, rows), jnp.float32),
        (force, *prepared, *parts),
        [pltpu.VMEM((total, 2 * count), jnp.bfloat16)] * 2,
        flops=4 * rows * total * 2 * count,
    )
    return out.reshape(rows)


def on_device(
    mode_shapes,
    unbalance,
    connectivity,
    stress_weights,
    face_low_nodes,
    face_high_nodes,
    natural_freq,
    damping_ratio,
    coupling,
    speed_index,
):
    count = natural_freq.shape[0]
    product = jnp.dot(unbalance, mode_shapes, preferred_element_type=jnp.float32)
    force = jnp.stack(
        [product[0, :count] - product[1, count:], product[0, count:] + product[1, :count]]
    )
    force = sum_over_slabs(force)
    speeds = speed_index
    for pairs in ([(0, 1), (1, 0), (2, 3), (3, 2)], [(0, 3), (3, 0), (1, 2), (2, 1)]):
        speeds = jnp.concatenate([speeds, lax.ppermute(speeds, "spd", pairs)])
    prepared = prepare(speeds, natural_freq, damping_ratio, coupling)
    below = from_behind(gather_rows(face_high_nodes, mode_shapes), "slab", 1)
    above = from_behind(gather_rows(face_low_nodes, mode_shapes), "slab", -1)
    parts = stress_modes_of(connectivity, stress_weights, below, mode_shapes, above)
    return peaks(force, prepared, parts)


def solution(mesh):
    return jax.shard_map(
        on_device,
        mesh=mesh,
        in_specs=(
            P("slab", None),
            P(None, "slab"),
            P(None, "slab"),
            P(None, "slab"),
            P("slab"),
            P("slab"),
            P(),
            P(),
            P(),
            P("spd"),
        ),
        out_specs=P("slab"),
        check_vma=False,
    )
```

```python
import functools
import math

import jax
import jax.numpy as jnp
from jax import lax
from jax.experimental import pallas as pl
from jax.experimental.pallas import tpu as pltpu
from jax.sharding import PartitionSpec as P

ITERS = 6
NGRID = 4096
X, Y, Z, CORES = 4, 4, 8, 2
BLOCK = 256
WINDOW = 1280
CODE = 64
ROOM0 = 50
MICRO = 3.0
bf16 = jnp.bfloat16
f32 = jnp.float32


def mm(a, b):
    return jnp.dot(a, b, preferred_element_type=f32)


VMEM = pl.BlockSpec(memory_space=pltpu.VMEM)
SMEM = pl.BlockSpec(memory_space=pltpu.SMEM)
HBM = pl.BlockSpec(memory_space=pltpu.HBM)


def call(body, out_shape, operands, scratch=(), specs=None, microseconds=1.0, room=24):
    return pl.pallas_call(
        body,
        out_shape=out_shape,
        in_specs=specs or [VMEM] * len(operands),
        out_specs=[VMEM] * len(out_shape),
        scratch_shapes=list(scratch),
        compiler_params=pltpu.CompilerParams(vmem_limit_bytes=room << 20),
        cost_estimate=pl.CostEstimate(flops=int(1e9 * microseconds), bytes_accessed=0, transcendentals=0),
    )(*operands)


def sds(shape, dtype):
    return jax.ShapeDtypeStruct(shape, dtype)


def slab_of(x, z, c):
    return (x * Z + z) * CORES + c


def slab_pairs(partner):
    return [
        (slab_of(x, z, c), slab_of(*partner(x, z, c)))
        for x in range(X)
        for z in range(Z)
        for c in range(CORES)
    ]


CORE_PAIRS = slab_pairs(lambda x, z, c: (x, z, 1 - c))


def odd_round(partner, mirror=lambda y: y ^ 1):
    pairs = []
    for x in range(X):
        for z in range(Z):
            for y in range(Y):
                pairs.append((slab_of(x, z, 0) * Y + y, slab_of(x, z, 0) * Y + mirror(y)))
                pairs.append((slab_of(x, z, 1) * Y + y, slab_of(*partner(x, z), 1) * Y + y))
    return sorted(pairs)


ROUNDS = (
    odd_round(lambda x, z: (x ^ 1, z)),
    odd_round(lambda x, z: (3 - x, z), lambda y: 3 - y),
    odd_round(lambda x, z: (x, z ^ 1)),
    odd_round(lambda x, z: (x, z ^ 2)),
    odd_round(lambda x, z: (x, 7 - z)),
)
N_SLAB = X * Z * CORES
FAR_PAIRS = [
    (j * Y + y, (j + 1 if j % 2 else j - 1) * Y + y) if 0 < j < N_SLAB - 1 else (j * Y + y, j * Y + (y ^ 1))
    for j in range(N_SLAB)
    for y in range(Y)
]


def first_body(unbalance, shapes, message, shapes_t, landing, load, sems):
    rows, width = shapes.shape
    parts = sems.shape[0] - 1
    step = rows // parts
    load_copy = pltpu.make_async_copy(unbalance, load, sems.at[parts])
    load_copy.start()
    copies = []
    for p in range(parts):
        s = pl.ds(p * step, step)
        copy = pltpu.make_async_copy(shapes.at[s, :], landing.at[s, :], sems.at[p])
        copy.start()
        copies.append(copy)
    load_copy.wait()
    total = jnp.zeros((load.shape[0], width), f32)
    for p in range(parts):
        copies[p].wait()
        block = landing[p * step : (p + 1) * step, :]
        total += mm(load[:, p * step : (p + 1) * step], block)
        shapes_t[:, p * step : (p + 1) * step] = jnp.transpose(block)
    half = width // 2
    message[0:1, :] = total[0:1, :half] - total[1:2, half:]
    message[1:2, :] = total[0:1, half:] + total[1:2, :half]


def first(unbalance, shapes):
    rows, width = shapes.shape
    parts = 8
    return call(
        first_body,
        [sds((2, width // 2), f32), sds((width, rows), bf16)],
        (unbalance, shapes),
        [
            pltpu.VMEM((rows, width), bf16),
            pltpu.VMEM(unbalance.shape, bf16),
            pltpu.SemaphoreType.DMA((parts + 1,)),
        ],
        [HBM, HBM],
        1.5,
        ROOM0,
    )


def gather_rows(nodes, one, shapes_t, table):
    rows = shapes_t.shape[1]
    count = nodes.shape[1]
    here = jnp.broadcast_to(nodes.astype(jnp.int16), (16, count))
    row = lax.broadcasted_iota(jnp.int16, (16, count), 0)
    zero = jnp.zeros((16, count), bf16)
    for r in range(0, rows, 16):
        table[r : r + 16, :] = jnp.where(here == row + jnp.int16(r), one, zero)
    return mm(shapes_t[...], table[...]).astype(bf16)


def near_gather_body(place, message_in, low, high, shapes_t, message_out, out, table):
    width = shapes_t.shape[0]
    nodes = jnp.where(place[0] == 0, high[...], low[...])
    one = jnp.ones((16, nodes.shape[1]), bf16)
    out[:width, :] = gather_rows(nodes, one, shapes_t, table)
    index = message_in[3:4, :].astype(jnp.int32)
    coarse = index // CODE
    fine = index - coarse * CODE
    row = jnp.concatenate([coarse.astype(f32), fine.astype(f32)], 1)
    out[width:, :] = jnp.broadcast_to(row, (16, row.shape[1])).astype(bf16)
    message_out[...] = message_in[...]


def far_gather_body(place, message_in, low, high, shapes_t, message_out, out, table):
    nodes = jnp.where(place[0] == 0, low[...], high[...])
    one = jnp.full((16, nodes.shape[1]), jnp.where(place[1] == 0, 1.0, 0.0), f32).astype(bf16)
    out[...] = gather_rows(nodes, one, shapes_t, table)
    message_out[...] = message_in[...]


def fill_table(table, links, weights, start):
    corners, count = links.shape
    here = (links - start).astype(jnp.int16)
    here = [jnp.broadcast_to(here[k : k + 1, :], (16, count)) for k in range(corners)]
    value = [jnp.broadcast_to(weights[k : k + 1, :], (16, count)) for k in range(corners)]
    row = lax.broadcasted_iota(jnp.int16, (16, count), 0)
    for r in range(0, WINDOW, 16):
        at = row + jnp.int16(r)
        entry = jnp.zeros((16, count), bf16)
        for k in range(corners):
            entry = jnp.where(here[k] == at, value[k], entry)
        table[r : r + 16, :] = entry


def middle_body(force_in, links, weights, shapes_t, force_out, out, tables, *, blocks):
    for i, b in enumerate(blocks):
        s = slice(b * BLOCK, (b + 1) * BLOCK)
        fill_table(tables.at[i % 2], links[:, s], weights[:, s], b * BLOCK)
        start = (b - 2) * BLOCK
        modes = mm(shapes_t[:, start : start + WINDOW], tables[i % 2])
        out[:, i * BLOCK : (i + 1) * BLOCK] = modes.astype(bf16)
    force_out[...] = force_in[...]


def end_body(place, force_in, links, weights, shapes_t, halo, force_out, out, window, tables, *, low_core):
    width, rows = shapes_t.shape
    reach = halo.shape[1]
    own = 1024

    low = place[0] == low_core

    @pl.when(low)
    def _():
        window[:, :reach] = halo[:width, :]
        window[:, reach:] = shapes_t[:, :own]

    @pl.when(jnp.logical_not(low))
    def _():
        window[:, :own] = shapes_t[:, rows - own :]
        window[:, own:] = halo[:width, :]

    base = jnp.where(low, 0, rows - 2 * BLOCK)
    for i in range(2):
        start = pl.multiple_of(base + i * BLOCK, BLOCK)
        fill_table(tables.at[i], links[:, pl.ds(start, BLOCK)], weights[:, pl.ds(start, BLOCK)], start)
        modes = mm(window[:, i * BLOCK : i * BLOCK + WINDOW], tables[i])
        out[:, i * BLOCK : (i + 1) * BLOCK] = modes.astype(bf16)
    force_out[...] = force_in[...]


def split(x):
    high = x.astype(bf16)
    return high, (x - high.astype(f32)).astype(bf16)


def prepare_body(
    place, message_in, speeds, there, halo, freq, damping, coupling, message_out, u_re, u_im, omega_out, c_high, c_low
):
    count = freq.shape[1]
    total = u_re.shape[0]
    tail = halo[halo.shape[0] - 16 :, :].astype(f32)
    tail = tail[0:1, : total // 2] * CODE + tail[0:1, total // 2 :]
    odd = jnp.concatenate([speeds[...].astype(f32), tail], 1)
    even = jnp.concatenate([there[2:3, :], there[3:4, :]], 1)
    index = jnp.where(place[0] == 0, even, odd)
    message_out[...] = message_in[...]
    omega = 0.25 + 4.0 * index / NGRID
    omega = jnp.transpose(jnp.broadcast_to(omega, (8, total)))[:, 0:1]
    omega = jnp.broadcast_to(omega, (total, count))
    f = freq[...]
    zeta = damping[...]
    d_re = f * f - omega * omega
    d_im = 2.0 * (zeta * f) * omega
    scale = omega / (d_re * d_re + d_im * d_im)
    u_re[...] = d_re * scale
    u_im[...] = d_im * scale
    omega_out[...] = omega[:, :128]
    i = lax.broadcasted_iota(jnp.int32, (count, count), 0)
    j = lax.broadcasted_iota(jnp.int32, (count, count), 1)
    coupled = jnp.transpose(coupling[...]) * (zeta * f * (1.5 / math.sqrt(count)))
    c_high[...], c_low[...] = split(jnp.where(i == j, 0.0, coupled))


def prepare(place, message, speeds, there, halo, freq, damping, coupling):
    total, count = 2 * speeds.shape[1], freq.shape[0]
    operands = (place, message, speeds, there, halo, freq.reshape(1, count), damping.reshape(1, count), coupling)
    return call(
        prepare_body,
        [
            sds(message.shape, f32),
            sds((total, count), f32),
            sds((total, count), f32),
            sds((total, 128), f32),
            sds((count, count), bf16),
            sds((count, count), bf16),
        ],
        operands,
        specs=[SMEM] + [VMEM] * 7,
        microseconds=0.9,
    )


def solve_body(place, mine, other, u_re, u_im, omega, c_high, c_low, out):
    force = jnp.where(place[0] == 1, mine[...], other[...])
    f_re, f_im = force[0:1, :], force[1:2, :]
    ch, cl = c_high[...], c_low[...]

    def coupled(y):
        high, low = split(y)
        return mm(high, ch) + (mm(low, ch) + mm(high, cl))

    total, count = u_re.shape
    tile = 256
    tiles = [pl.ds(t, tile) for t in range(0, total, tile)]
    state = []
    for s in tiles:
        ur, ui = u_re[s, :], u_im[s, :]
        state.append((f_re * ur + f_im * ui, f_im * ur - f_re * ui))
    for sweep in range(ITERS):
        after = []
        for s, (yr, yi) in zip(tiles, state):
            pr, pi = coupled(yr), coupled(yi)
            ur, ui = u_re[s, :], u_im[s, :]
            top_re, top_im = f_re + pi, f_im - pr
            after.append((top_re * ur + top_im * ui, top_im * ur - top_re * ui))
        state = after
    for s, (yr, yi) in zip(tiles, state):
        w = jnp.concatenate([omega[s, :]] * (count // 128), 1)
        out[s, :count] = (yr * w).astype(bf16)
        out[s, count:] = (yi * w).astype(bf16)


def solve(place, mine, other, prepared):
    total, count = prepared[0].shape
    operands = (place, mine, other, *prepared)
    return call(
        solve_body, [sds((total, 2 * count), bf16)], operands, specs=[SMEM] + [VMEM] * 7, microseconds=4.0
    )[0]


def peaks_tile(coords, modes, for_re, for_im):
    total, twice = coords.shape
    tile = 256
    best = jnp.zeros((8, modes.shape[1]), f32)
    for s in range(0, total, tile):
        re = mm(for_re[s : s + tile, :], modes)
        im = mm(for_im[s : s + tile, :], modes)
        square = re * re + im * im
        best = jnp.maximum(best, jnp.max(square.reshape(tile // 8, 8, modes.shape[1]), axis=0))
    return best


def parts_of(parts):
    at = 0
    for part in parts:
        for e in range(0, part.shape[1], BLOCK):
            yield at, part, e
            at += BLOCK


def half_peaks_body(coords, far, middle_a, middle_b, near, best, for_re, for_im):
    spread(coords, for_re, for_im)
    for at, part, e in parts_of((far, middle_a, middle_b, near)):
        best[:, at : at + BLOCK] = peaks_tile(coords, part[:, e : e + BLOCK], for_re, for_im)


def spread(coords, for_re, for_im):
    count = coords.shape[1] // 2
    re, im = coords[:, :count], coords[:, count:]
    for_re[:, :count] = re
    for_re[:, count:] = -im
    for_im[:, :count] = im
    for_im[:, count:] = re


def all_peaks_body(place, coords, before, far, middle_a, middle_b, near, out, for_re, for_im):
    spread(coords, for_re, for_im)
    rows = out.shape[1]
    end = far.shape[1]
    even = place[0] == 0
    for at, part, e in parts_of((far, middle_a, middle_b, near)):
        best = jnp.maximum(before[:, at : at + BLOCK], peaks_tile(coords, part[:, e : e + BLOCK], for_re, for_im))
        peak = jnp.sqrt(jnp.max(best, axis=0, keepdims=True))
        to = at
        if part is far:
            to = jnp.where(even, at, at + rows - end)
        if part is near:
            to = jnp.where(even, at, at - rows + end)
        out[0:1, pl.ds(pl.multiple_of(to, BLOCK), BLOCK)] = peak


def peaks(place, coords, parts):
    total, twice = coords.shape
    rows = sum(p.shape[1] for p in parts)
    there = lax.ppermute(coords, "slab", CORE_PAIRS)
    scratch = [pltpu.VMEM((total, twice), bf16)] * 2
    best = call(half_peaks_body, [sds((8, rows), f32)], (coords, *parts), scratch, microseconds=2.5)[0]
    out = call(
        all_peaks_body,
        [sds((1, rows), f32)],
        (place, there, best, *parts),
        scratch,
        [SMEM] + [VMEM] * 6,
        2.5,
    )[0]
    return out.reshape(rows)


def on_device(
    mode_shapes,
    unbalance,
    connectivity,
    stress_weights,
    face_low_nodes,
    face_high_nodes,
    natural_freq,
    damping_ratio,
    coupling,
    speed_index,
):
    rows, width = mode_shapes.shape
    reach = face_low_nodes.shape[0]
    slab = lax.axis_index("slab")
    edge = jnp.logical_or(slab == 0, slab == N_SLAB - 1)
    place = jnp.stack([slab % CORES, edge.astype(jnp.int32)]).astype(jnp.int32)
    low = face_low_nodes.reshape(1, reach)
    high = face_high_nodes.reshape(1, reach)

    speeds = speed_index.reshape(1, -1)
    force, shapes_t = first(unbalance, mode_shapes)
    small = sds((2, width // 2), f32)
    letter = sds((4, width // 2), f32)
    tables = pltpu.VMEM((2, WINDOW, BLOCK), bf16)
    table = pltpu.VMEM((rows, reach), bf16)

    def swap(x, number):
        return lax.ppermute(x, ("slab", "spd"), ROUNDS[number])

    def middle(blocks, force):
        return call(
            functools.partial(middle_body, blocks=blocks),
            [sds(force.shape, f32), sds((width, len(blocks) * BLOCK), bf16)],
            (force, connectivity, stress_weights, shapes_t),
            [tables],
            microseconds=MICRO * 1.2,
        )

    def end(halo, low_core, force):
        return call(
            functools.partial(end_body, low_core=low_core),
            [small, sds((width, 2 * BLOCK), bf16)],
            (place, force, connectivity, stress_weights, shapes_t, halo),
            [pltpu.VMEM((width, 3 * reach), bf16), tables],
            [SMEM] + [VMEM] * 5,
            MICRO * 1.6,
        )

    arrived = lax.ppermute(force, "slab", CORE_PAIRS)
    force, far_rows = call(
        far_gather_body,
        [small, sds((width, reach), bf16)],
        (place, force, low, high, shapes_t),
        [table],
        [SMEM] + [VMEM] * 4,
        MICRO * 1.8,
    )
    far_halo = lax.ppermute(far_rows, ("slab", "spd"), FAR_PAIRS)
    own = speeds.astype(f32)
    message = jnp.concatenate([force + arrived, own, own])
    arrived = swap(message, 0)
    message, middle_a = middle((2, 3), message)
    message = jnp.concatenate([message[:2] + arrived[:2], message[2:3], arrived[2:3]])
    there = swap(message, 1)
    message, near_rows = call(
        near_gather_body,
        [letter, sds((width + 16, reach), bf16)],
        (place, message, low, high, shapes_t),
        [table],
        [SMEM] + [VMEM] * 4,
        MICRO * 1.8,
    )
    near_halo = lax.ppermute(near_rows, "slab", CORE_PAIRS)
    force = message[:2] + there[:2]
    arrived = swap(force, 2)
    force, middle_b = middle((4, 5), force)
    force = force + arrived
    arrived = swap(force, 3)
    force, near = end(near_halo, 1, force)
    force, *prepared = prepare(place, force, speeds, there, near_halo, natural_freq, damping_ratio, coupling)
    force = force + arrived
    arrived = swap(force, 4)
    force, far = end(far_halo, 0, force)
    force = force + arrived
    coords = solve(place, force, lax.ppermute(force, "slab", CORE_PAIRS), prepared)
    return peaks(place, coords, (far, middle_a, middle_b, near))


def solution(mesh):
    return jax.shard_map(
        on_device,
        mesh=mesh,
        in_specs=(
            P("slab", None),
            P(None, "slab"),
            P(None, "slab"),
            P(None, "slab"),
            P("slab"),
            P("slab"),
            P(),
            P(),
            P(),
            P("spd"),
        ),
        out_specs=P("slab"),
        check_vma=False,
    )
```

```python
import functools
import math

import jax
import jax.numpy as jnp
from jax import lax
from jax.experimental import pallas as pl
from jax.experimental.pallas import tpu as pltpu
from jax.sharding import PartitionSpec as P

ITERS = 6
EARLY = 4
NGRID = 4096
X, Y, Z, CORES = 4, 4, 8, 2
BLOCK = 256
WINDOW = 1280
CODE = 64
ROOM0 = 50
MICRO = 3.0
bf16 = jnp.bfloat16
f32 = jnp.float32


def mm(a, b):
    return jnp.dot(a, b, preferred_element_type=f32)


VMEM = pl.BlockSpec(memory_space=pltpu.VMEM)
SMEM = pl.BlockSpec(memory_space=pltpu.SMEM)
HBM = pl.BlockSpec(memory_space=pltpu.HBM)


def call(body, out_shape, operands, scratch=(), specs=None, microseconds=1.0, room=24):
    return pl.pallas_call(
        body,
        out_shape=out_shape,
        in_specs=specs or [VMEM] * len(operands),
        out_specs=[VMEM] * len(out_shape),
        scratch_shapes=list(scratch),
        compiler_params=pltpu.CompilerParams(vmem_limit_bytes=int(room * 2**20)),
        cost_estimate=pl.CostEstimate(flops=int(1e9 * microseconds), bytes_accessed=0, transcendentals=0),
    )(*operands)


def sds(shape, dtype):
    return jax.ShapeDtypeStruct(shape, dtype)


def slab_of(x, z, c):
    return (x * Z + z) * CORES + c


def slab_pairs(partner):
    return [
        (slab_of(x, z, c), slab_of(*partner(x, z, c)))
        for x in range(X)
        for z in range(Z)
        for c in range(CORES)
    ]


CORE_PAIRS = slab_pairs(lambda x, z, c: (x, z, 1 - c))


def odd_round(partner, mirror=lambda y: y ^ 1):
    pairs = []
    for x in range(X):
        for z in range(Z):
            for y in range(Y):
                pairs.append((slab_of(x, z, 0) * Y + y, slab_of(x, z, 0) * Y + mirror(y)))
                pairs.append((slab_of(x, z, 1) * Y + y, slab_of(*partner(x, z), 1) * Y + y))
    return sorted(pairs)


ROUNDS = (
    odd_round(lambda x, z: (x ^ 1, z)),
    odd_round(lambda x, z: (3 - x, z), lambda y: 3 - y),
    odd_round(lambda x, z: (x, z ^ 1)),
    odd_round(lambda x, z: (x, z ^ 2)),
    odd_round(lambda x, z: (x, 7 - z)),
)
N_SLAB = X * Z * CORES
FAR_PAIRS = [
    (j * Y + y, (j + 1 if j % 2 else j - 1) * Y + y) if 0 < j < N_SLAB - 1 else (j * Y + y, j * Y + (y ^ 1))
    for j in range(N_SLAB)
    for y in range(Y)
]


def first_body(unbalance, shapes, message, shapes_t, landing, load, sems):
    rows, width = shapes.shape
    parts = sems.shape[0] - 1
    step = rows // parts
    load_copy = pltpu.make_async_copy(unbalance, load, sems.at[parts])
    load_copy.start()
    copies = []
    for p in range(parts):
        s = pl.ds(p * step, step)
        copy = pltpu.make_async_copy(shapes.at[s, :], landing.at[s, :], sems.at[p])
        copy.start()
        copies.append(copy)
    load_copy.wait()
    total = jnp.zeros((load.shape[0], width), f32)
    for p in range(parts):
        copies[p].wait()
        block = landing[p * step : (p + 1) * step, :]
        total += mm(load[:, p * step : (p + 1) * step], block)
        shapes_t[:, p * step : (p + 1) * step] = jnp.transpose(block)
    half = width // 2
    message[0:1, :] = total[0:1, :half] - total[1:2, half:]
    message[1:2, :] = total[0:1, half:] + total[1:2, :half]


def first(unbalance, shapes):
    rows, width = shapes.shape
    parts = 4
    return call(
        first_body,
        [sds((2, width // 2), f32), sds((width, rows), bf16)],
        (unbalance, shapes),
        [
            pltpu.VMEM((rows, width), bf16),
            pltpu.VMEM(unbalance.shape, bf16),
            pltpu.SemaphoreType.DMA((parts + 1,)),
        ],
        [HBM, HBM],
        1.5,
        ROOM0,
    )


def gather_rows(nodes, one, shapes_t, table):
    rows = shapes_t.shape[1]
    count = nodes.shape[1]
    here = jnp.broadcast_to(nodes.astype(jnp.int16), (16, count))
    row = lax.broadcasted_iota(jnp.int16, (16, count), 0)
    zero = jnp.zeros((16, count), bf16)
    for r in range(0, rows, 16):
        table[r : r + 16, :] = jnp.where(here == row + jnp.int16(r), one, zero)
    return mm(shapes_t[...], table[...]).astype(bf16)


def near_gather_body(place, message_in, low, high, shapes_t, message_out, out, table):
    width = shapes_t.shape[0]
    nodes = jnp.where(place[0] == 0, high[...], low[...])
    one = jnp.ones((16, nodes.shape[1]), bf16)
    out[:width, :] = gather_rows(nodes, one, shapes_t, table)
    index = message_in[3:4, :].astype(jnp.int32)
    coarse = index // CODE
    fine = index - coarse * CODE
    row = jnp.concatenate([coarse.astype(f32), fine.astype(f32)], 1)
    out[width:, :] = jnp.broadcast_to(row, (16, row.shape[1])).astype(bf16)
    message_out[...] = message_in[...]


def far_gather_body(place, message_in, low, high, shapes_t, message_out, out, table):
    nodes = jnp.where(place[0] == 0, low[...], high[...])
    one = jnp.full((16, nodes.shape[1]), jnp.where(place[1] == 0, 1.0, 0.0), f32).astype(bf16)
    out[...] = gather_rows(nodes, one, shapes_t, table)
    message_out[...] = message_in[...]


def fill_table(table, links, weights, start):
    corners, count = links.shape
    here = (links - start).astype(jnp.int16)
    here = [jnp.broadcast_to(here[k : k + 1, :], (16, count)) for k in range(corners)]
    value = [jnp.broadcast_to(weights[k : k + 1, :], (16, count)) for k in range(corners)]
    row = lax.broadcasted_iota(jnp.int16, (16, count), 0)
    for r in range(0, WINDOW, 16):
        at = row + jnp.int16(r)
        entry = jnp.zeros((16, count), bf16)
        for k in range(corners):
            entry = jnp.where(here[k] == at, value[k], entry)
        table[r : r + 16, :] = entry


def middle_body(force_in, links, weights, shapes_t, force_out, out, tables, *, blocks):
    for i, b in enumerate(blocks):
        s = slice(b * BLOCK, (b + 1) * BLOCK)
        fill_table(tables.at[i % 2], links[:, s], weights[:, s], b * BLOCK)
        start = (b - 2) * BLOCK
        modes = mm(shapes_t[:, start : start + WINDOW], tables[i % 2])
        out[:, i * BLOCK : (i + 1) * BLOCK] = modes.astype(bf16)
    force_out[...] = force_in[...]


def end_body(place, force_in, links, weights, shapes_t, halo, force_out, out, window, tables, *, low_core):
    width, rows = shapes_t.shape
    reach = halo.shape[1]
    own = 1024

    low = place[0] == low_core

    @pl.when(low)
    def _():
        window[:, :reach] = halo[:width, :]
        window[:, reach:] = shapes_t[:, :own]

    @pl.when(jnp.logical_not(low))
    def _():
        window[:, :own] = shapes_t[:, rows - own :]
        window[:, own:] = halo[:width, :]

    base = jnp.where(low, 0, rows - 2 * BLOCK)
    for i in range(2):
        start = pl.multiple_of(base + i * BLOCK, BLOCK)
        fill_table(tables.at[i], links[:, pl.ds(start, BLOCK)], weights[:, pl.ds(start, BLOCK)], start)
        modes = mm(window[:, i * BLOCK : i * BLOCK + WINDOW], tables[i])
        out[:, i * BLOCK : (i + 1) * BLOCK] = modes.astype(bf16)
    force_out[...] = force_in[...]


def split(x):
    high = x.astype(bf16)
    return high, (x - high.astype(f32)).astype(bf16)


def prepare_body(
    place, message_in, speeds, there, halo, freq, damping, coupling, message_out, u_re, u_im, omega_out, c_high, c_low
):
    count = freq.shape[1]
    total = u_re.shape[0]
    tail = halo[halo.shape[0] - 16 :, :].astype(f32)
    tail = tail[0:1, : total // 2] * CODE + tail[0:1, total // 2 :]
    odd = jnp.concatenate([speeds[...].astype(f32), tail], 1)
    even = jnp.concatenate([there[2:3, :], there[3:4, :]], 1)
    index = jnp.where(place[0] == 0, even, odd)
    message_out[...] = message_in[...]
    omega = 0.25 + 4.0 * index / NGRID
    omega = jnp.transpose(jnp.broadcast_to(omega, (8, total)))[:, 0:1]
    omega = jnp.broadcast_to(omega, (total, count))
    f = freq[...]
    zeta = damping[...]
    d_re = f * f - omega * omega
    d_im = 2.0 * (zeta * f) * omega
    scale = omega / (d_re * d_re + d_im * d_im)
    u_re[...] = d_re * scale
    u_im[...] = d_im * scale
    omega_out[...] = omega[:, :128]
    i = lax.broadcasted_iota(jnp.int32, (count, count), 0)
    j = lax.broadcasted_iota(jnp.int32, (count, count), 1)
    coupled = jnp.transpose(coupling[...]) * (zeta * f * (1.5 / math.sqrt(count)))
    c_high[...], c_low[...] = split(jnp.where(i == j, 0.0, coupled))


def prepare(place, message, speeds, there, halo, freq, damping, coupling):
    total, count = 2 * speeds.shape[1], freq.shape[0]
    operands = (place, message, speeds, there, halo, freq.reshape(1, count), damping.reshape(1, count), coupling)
    return call(
        prepare_body,
        [
            sds(message.shape, f32),
            sds((total, count), f32),
            sds((total, count), f32),
            sds((total, 128), f32),
            sds((count, count), bf16),
            sds((count, count), bf16),
        ],
        operands,
        specs=[SMEM] + [VMEM] * 7,
        microseconds=0.9,
    )


def solve_body(place, mine, other, u_re, u_im, omega, c_high, c_low, out):
    force = jnp.where(place[0] == 1, mine[...], other[...])
    f_re, f_im = force[0:1, :], force[1:2, :]
    ch, cl = c_high[...], c_low[...]

    def coupled(y, sweep):
        if sweep < EARLY:
            return mm(y.astype(bf16), ch)
        high, low = split(y)
        return mm(high, ch) + (mm(low, ch) + mm(high, cl))

    total, count = u_re.shape
    tile = 256
    tiles = [pl.ds(t, tile) for t in range(0, total, tile)]
    state = []
    for s in tiles:
        ur, ui = u_re[s, :], u_im[s, :]
        state.append((f_re * ur + f_im * ui, f_im * ur - f_re * ui))
    for sweep in range(ITERS):
        after = []
        for s, (yr, yi) in zip(tiles, state):
            pr, pi = coupled(yr, sweep), coupled(yi, sweep)
            ur, ui = u_re[s, :], u_im[s, :]
            top_re, top_im = f_re + pi, f_im - pr
            after.append((top_re * ur + top_im * ui, top_im * ur - top_re * ui))
        state = after
    for s, (yr, yi) in zip(tiles, state):
        w = jnp.concatenate([omega[s, :]] * (count // 128), 1)
        out[s, :count] = (yr * w).astype(bf16)
        out[s, count:] = (yi * w).astype(bf16)


def solve(place, mine, other, prepared):
    total, count = prepared[0].shape
    operands = (place, mine, other, *prepared)
    return call(
        solve_body, [sds((total, 2 * count), bf16)], operands, specs=[SMEM] + [VMEM] * 7, microseconds=4.0
    )[0]


def peaks_tile(coords, modes, for_re, for_im):
    total, twice = coords.shape
    tile = 256
    best = jnp.zeros((8, modes.shape[1]), f32)
    for s in range(0, total, tile):
        re = mm(for_re[s : s + tile, :], modes)
        im = mm(for_im[s : s + tile, :], modes)
        square = re * re + im * im
        best = jnp.maximum(best, jnp.max(square.reshape(tile // 8, 8, modes.shape[1]), axis=0))
    return best


def parts_of(parts):
    at = 0
    for part in parts:
        for e in range(0, part.shape[1], BLOCK):
            yield at, part, e
            at += BLOCK


def half_peaks_body(coords, far, middle_a, middle_b, near, best, for_re, for_im):
    spread(coords, for_re, for_im)
    for at, part, e in parts_of((far, middle_a, middle_b, near)):
        best[:, at : at + BLOCK] = peaks_tile(coords, part[:, e : e + BLOCK], for_re, for_im)


def spread(coords, for_re, for_im):
    count = coords.shape[1] // 2
    re, im = coords[:, :count], coords[:, count:]
    for_re[:, :count] = re
    for_re[:, count:] = -im
    for_im[:, :count] = im
    for_im[:, count:] = re


def all_peaks_body(place, coords, before, far, middle_a, middle_b, near, out, for_re, for_im):
    spread(coords, for_re, for_im)
    rows = out.shape[1]
    end = far.shape[1]
    even = place[0] == 0
    for at, part, e in parts_of((far, middle_a, middle_b, near)):
        best = jnp.maximum(before[:, at : at + BLOCK], peaks_tile(coords, part[:, e : e + BLOCK], for_re, for_im))
        peak = jnp.sqrt(jnp.max(best, axis=0, keepdims=True))
        to = at
        if part is far:
            to = jnp.where(even, at, at + rows - end)
        if part is near:
            to = jnp.where(even, at, at - rows + end)
        out[0:1, pl.ds(pl.multiple_of(to, BLOCK), BLOCK)] = peak


def peaks(place, coords, parts):
    total, twice = coords.shape
    rows = sum(p.shape[1] for p in parts)
    there = lax.ppermute(coords, "slab", CORE_PAIRS)
    scratch = [pltpu.VMEM((total, twice), bf16)] * 2
    best = call(half_peaks_body, [sds((8, rows), f32)], (coords, *parts), scratch, microseconds=2.5)[0]
    out = call(
        all_peaks_body,
        [sds((1, rows), f32)],
        (place, there, best, *parts),
        scratch,
        [SMEM] + [VMEM] * 6,
        2.5,
    )[0]
    return out.reshape(rows)


def on_device(
    mode_shapes,
    unbalance,
    connectivity,
    stress_weights,
    face_low_nodes,
    face_high_nodes,
    natural_freq,
    damping_ratio,
    coupling,
    speed_index,
):
    rows, width = mode_shapes.shape
    reach = face_low_nodes.shape[0]
    slab = lax.axis_index("slab")
    edge = jnp.logical_or(slab == 0, slab == N_SLAB - 1)
    place = jnp.stack([slab % CORES, edge.astype(jnp.int32)]).astype(jnp.int32)
    low = face_low_nodes.reshape(1, reach)
    high = face_high_nodes.reshape(1, reach)

    speeds = speed_index.reshape(1, -1)
    force, shapes_t = first(unbalance, mode_shapes)
    small = sds((2, width // 2), f32)
    letter = sds((4, width // 2), f32)
    tables = pltpu.VMEM((2, WINDOW, BLOCK), bf16)
    table = pltpu.VMEM((rows, reach), bf16)

    def swap(x, number):
        return lax.ppermute(x, ("slab", "spd"), ROUNDS[number])

    def middle(blocks, force):
        return call(
            functools.partial(middle_body, blocks=blocks),
            [sds(force.shape, f32), sds((width, len(blocks) * BLOCK), bf16)],
            (force, connectivity, stress_weights, shapes_t),
            [tables],
            microseconds=MICRO * 1.2,
        )

    def end(halo, low_core, force):
        return call(
            functools.partial(end_body, low_core=low_core),
            [small, sds((width, 2 * BLOCK), bf16)],
            (place, force, connectivity, stress_weights, shapes_t, halo),
            [pltpu.VMEM((width, 3 * reach), bf16), tables],
            [SMEM] + [VMEM] * 5,
            MICRO * 1.6,
        )

    arrived = lax.ppermute(force, "slab", CORE_PAIRS)
    force, middle_a = middle((2, 3), force)
    own = speeds.astype(f32)
    message = jnp.concatenate([force + arrived, own, own])
    arrived = swap(message, 0)
    message, far_rows = call(
        far_gather_body,
        [letter, sds((width, reach), bf16)],
        (place, message, low, high, shapes_t),
        [table],
        [SMEM] + [VMEM] * 4,
        MICRO * 1.8,
    )
    far_halo = lax.ppermute(far_rows, ("slab", "spd"), FAR_PAIRS)
    message = jnp.concatenate([message[:2] + arrived[:2], message[2:3], arrived[2:3]])
    there = swap(message, 1)
    message, near_rows = call(
        near_gather_body,
        [letter, sds((width + 16, reach), bf16)],
        (place, message, low, high, shapes_t),
        [table],
        [SMEM] + [VMEM] * 4,
        MICRO * 1.8,
    )
    near_halo = lax.ppermute(near_rows, "slab", CORE_PAIRS)
    force = message[:2] + there[:2]
    arrived = swap(force, 2)
    force, middle_b = middle((4, 5), force)
    force = force + arrived
    arrived = swap(force, 3)
    force, near = end(near_halo, 1, force)
    force = force + arrived
    arrived = swap(force, 4)
    force, far = end(far_halo, 0, force)
    force, *prepared = prepare(place, force, speeds, there, near_halo, natural_freq, damping_ratio, coupling)
    force = force + arrived
    coords = solve(place, force, lax.ppermute(force, "slab", CORE_PAIRS), prepared)
    return peaks(place, coords, (far, middle_a, middle_b, near))


def solution(mesh):
    return jax.shard_map(
        on_device,
        mesh=mesh,
        in_specs=(
            P("slab", None),
            P(None, "slab"),
            P(None, "slab"),
            P(None, "slab"),
            P("slab"),
            P("slab"),
            P(),
            P(),
            P(),
            P("spd"),
        ),
        out_specs=P("slab"),
        check_vma=False,
    )
```

```python
import functools
import math

import jax
import jax.numpy as jnp
from jax import lax
from jax.experimental import pallas as pl
from jax.experimental.pallas import tpu as pltpu
from jax.sharding import PartitionSpec as P

ITERS = 6
EARLY = 4
NGRID = 4096
X, Y, Z, CORES = 4, 4, 8, 2
BLOCK = 256
WINDOW = 1280
CODE = 64
ROOM0 = 50
MICRO = 8.0
bf16 = jnp.bfloat16
f32 = jnp.float32


def mm(a, b):
    return jnp.dot(a, b, preferred_element_type=f32)


VMEM = pl.BlockSpec(memory_space=pltpu.VMEM)
HBM = pl.BlockSpec(memory_space=pltpu.HBM)


def call(body, out_shape, operands, scratch=(), specs=None, microseconds=1.0, room=24):
    return pl.pallas_call(
        body,
        out_shape=out_shape,
        in_specs=specs or [VMEM] * len(operands),
        out_specs=[VMEM] * len(out_shape),
        scratch_shapes=list(scratch),
        compiler_params=pltpu.CompilerParams(vmem_limit_bytes=int(room * 2**20)),
        cost_estimate=pl.CostEstimate(flops=int(1e9 * microseconds), bytes_accessed=0, transcendentals=0),
    )(*operands)


def sds(shape, dtype):
    return jax.ShapeDtypeStruct(shape, dtype)


def odd_core():
    return lax.rem(lax.axis_index("slab"), CORES)


def end_slab():
    slab = lax.axis_index("slab")
    return jnp.logical_or(slab == 0, slab == N_SLAB - 1)


def slab_of(x, z, c):
    return (x * Z + z) * CORES + c


def slab_pairs(partner):
    return [
        (slab_of(x, z, c), slab_of(*partner(x, z, c)))
        for x in range(X)
        for z in range(Z)
        for c in range(CORES)
    ]


CORE_PAIRS = slab_pairs(lambda x, z, c: (x, z, 1 - c))


def odd_round(partner, mirror=lambda y: y ^ 1):
    pairs = []
    for x in range(X):
        for z in range(Z):
            for y in range(Y):
                pairs.append((slab_of(x, z, 0) * Y + y, slab_of(x, z, 0) * Y + mirror(y)))
                pairs.append((slab_of(x, z, 1) * Y + y, slab_of(*partner(x, z), 1) * Y + y))
    return sorted(pairs)


ROUNDS = (
    odd_round(lambda x, z: (x ^ 1, z)),
    odd_round(lambda x, z: (3 - x, z), lambda y: 3 - y),
    odd_round(lambda x, z: (x, z ^ 1)),
    odd_round(lambda x, z: (x, z ^ 2)),
    odd_round(lambda x, z: (x, 7 - z)),
)
N_SLAB = X * Z * CORES
FAR_PAIRS = [
    (j * Y + y, (j + 1 if j % 2 else j - 1) * Y + y) if 0 < j < N_SLAB - 1 else (j * Y + y, j * Y + (y ^ 1))
    for j in range(N_SLAB)
    for y in range(Y)
]


def first_body(unbalance, shapes, message, shapes_t, landing, load, sems):
    rows, width = shapes.shape
    parts = sems.shape[0] - 1
    step = rows // parts
    load_copy = pltpu.make_async_copy(unbalance, load, sems.at[parts])
    load_copy.start()
    copies = []
    for p in range(parts):
        s = pl.ds(p * step, step)
        copy = pltpu.make_async_copy(shapes.at[s, :], landing.at[s, :], sems.at[p])
        copy.start()
        copies.append(copy)
    load_copy.wait()
    total = jnp.zeros((load.shape[0], width), f32)
    for p in range(parts):
        copies[p].wait()
        block = landing[p * step : (p + 1) * step, :]
        total += mm(load[:, p * step : (p + 1) * step], block)
        shapes_t[:, p * step : (p + 1) * step] = jnp.transpose(block)
    half = width // 2
    message[0:1, :] = total[0:1, :half] - total[1:2, half:]
    message[1:2, :] = total[0:1, half:] + total[1:2, :half]


def first(unbalance, shapes):
    rows, width = shapes.shape
    parts = 4
    return call(
        first_body,
        [sds((2, width // 2), f32), sds((width, rows), bf16)],
        (unbalance, shapes),
        [
            pltpu.VMEM((rows, width), bf16),
            pltpu.VMEM(unbalance.shape, bf16),
            pltpu.SemaphoreType.DMA((parts + 1,)),
        ],
        [HBM, HBM],
        1.5,
        ROOM0,
    )


def gather_rows(nodes, one, shapes_t, table):
    rows = shapes_t.shape[1]
    count = nodes.shape[1]
    here = jnp.broadcast_to(nodes.astype(jnp.int16), (16, count))
    row = lax.broadcasted_iota(jnp.int16, (16, count), 0)
    zero = jnp.zeros((16, count), bf16)
    for r in range(0, rows, 16):
        table[r : r + 16, :] = jnp.where(here == row + jnp.int16(r), one, zero)
    return mm(shapes_t[...], table[...]).astype(bf16)


def near_gather_body(message_in, speeds, low, high, shapes_t, message_out, out, table):
    width = shapes_t.shape[0]
    nodes = jnp.where(odd_core() == 0, high[...], low[...])
    one = jnp.ones((16, nodes.shape[1]), bf16)
    out[:width, :] = gather_rows(nodes, one, shapes_t, table)
    index = speeds[...].astype(jnp.int32)
    coarse = index // CODE
    fine = index - coarse * CODE
    row = jnp.concatenate([coarse.astype(f32), fine.astype(f32)], 1)
    out[width:, :] = jnp.broadcast_to(row, (16, row.shape[1])).astype(bf16)
    message_out[...] = message_in[...]


def far_gather_body(message_in, low, high, shapes_t, message_out, out, table):
    nodes = jnp.where(odd_core() == 0, low[...], high[...])
    one = jnp.full((16, nodes.shape[1]), jnp.where(end_slab(), 0.0, 1.0), f32).astype(bf16)
    out[...] = gather_rows(nodes, one, shapes_t, table)
    message_out[...] = message_in[...]


def fill_table(table, links, weights, start):
    corners, count = links.shape
    here = (links - start).astype(jnp.int16)
    here = [jnp.broadcast_to(here[k : k + 1, :], (16, count)) for k in range(corners)]
    value = [jnp.broadcast_to(weights[k : k + 1, :], (16, count)) for k in range(corners)]
    row = lax.broadcasted_iota(jnp.int16, (16, count), 0)
    for r in range(0, WINDOW, 16):
        at = row + jnp.int16(r)
        entry = jnp.zeros((16, count), bf16)
        for k in range(corners):
            entry = jnp.where(here[k] == at, value[k], entry)
        table[r : r + 16, :] = entry


def middle_body(force_in, links, weights, shapes_t, force_out, out, tables, *, blocks):
    for i, b in enumerate(blocks):
        s = slice(b * BLOCK, (b + 1) * BLOCK)
        fill_table(tables.at[i % 2], links[:, s], weights[:, s], b * BLOCK)
        start = (b - 2) * BLOCK
        modes = mm(shapes_t[:, start : start + WINDOW], tables[i % 2])
        out[:, i * BLOCK : (i + 1) * BLOCK] = modes.astype(bf16)
    force_out[...] = force_in[...]


def end_body(force_in, links, weights, shapes_t, halo, force_out, out, window, tables, *, low_core):
    width, rows = shapes_t.shape
    reach = halo.shape[1]
    own = 1024

    low = odd_core() == low_core

    @pl.when(low)
    def _():
        window[:, :reach] = halo[:width, :]
        window[:, reach:] = shapes_t[:, :own]

    @pl.when(jnp.logical_not(low))
    def _():
        window[:, :own] = shapes_t[:, rows - own :]
        window[:, own:] = halo[:width, :]

    base = jnp.where(low, 0, rows - 2 * BLOCK)
    for i in range(2):
        start = pl.multiple_of(base + i * BLOCK, BLOCK)
        fill_table(tables.at[i], links[:, pl.ds(start, BLOCK)], weights[:, pl.ds(start, BLOCK)], start)
        modes = mm(window[:, i * BLOCK : i * BLOCK + WINDOW], tables[i])
        out[:, i * BLOCK : (i + 1) * BLOCK] = modes.astype(bf16)
    force_out[...] = force_in[...]


def split(x):
    high = x.astype(bf16)
    return high, (x - high.astype(f32)).astype(bf16)


def prepare_body(
    message_in, speeds, there, halo, freq, damping, coupling, message_out, u_re, u_im, omega_out, c_high, c_low
):
    count = freq.shape[1]
    total = u_re.shape[0]
    tail = halo[halo.shape[0] - 16 :, :].astype(f32)
    tail = tail[0:1, : total // 2] * CODE + tail[0:1, total // 2 :]
    odd = jnp.concatenate([speeds[...].astype(f32), tail], 1)
    even = jnp.concatenate([there[2:3, :], there[3:4, :]], 1)
    index = jnp.where(odd_core() == 0, even, odd)
    message_out[...] = message_in[...]
    omega = 0.25 + 4.0 * index / NGRID
    omega = jnp.transpose(jnp.broadcast_to(omega, (8, total)))[:, 0:1]
    omega = jnp.broadcast_to(omega, (total, count))
    f = freq[...]
    zeta = damping[...]
    d_re = f * f - omega * omega
    d_im = 2.0 * (zeta * f) * omega
    scale = omega / (d_re * d_re + d_im * d_im)
    u_re[...] = d_re * scale
    u_im[...] = d_im * scale
    omega_out[...] = omega[:, :128]
    i = lax.broadcasted_iota(jnp.int32, (count, count), 0)
    j = lax.broadcasted_iota(jnp.int32, (count, count), 1)
    coupled = jnp.transpose(coupling[...]) * (zeta * f * (1.5 / math.sqrt(count)))
    c_high[...], c_low[...] = split(jnp.where(i == j, 0.0, coupled))


def prepare(message, speeds, there, halo, freq, damping, coupling):
    total, count = 2 * speeds.shape[1], freq.shape[0]
    operands = (message, speeds, there, halo, freq.reshape(1, count), damping.reshape(1, count), coupling)
    return call(
        prepare_body,
        [
            sds(message.shape, f32),
            sds((total, count), f32),
            sds((total, count), f32),
            sds((total, 128), f32),
            sds((count, count), bf16),
            sds((count, count), bf16),
        ],
        operands,
        specs=[VMEM] * 7,
        microseconds=0.9,
    )


def solve_body(mine, other, u_re, u_im, omega, c_high, c_low, for_re, for_im):
    force = jnp.where(odd_core() == 1, mine[...], other[...])
    f_re, f_im = force[0:1, :], force[1:2, :]
    ch, cl = c_high[...], c_low[...]

    def coupled(y, sweep):
        if sweep < EARLY:
            return mm(y.astype(bf16), ch)
        high, low = split(y)
        return mm(high, ch) + (mm(low, ch) + mm(high, cl))

    total, count = u_re.shape
    tile = 256
    tiles = [pl.ds(t, tile) for t in range(0, total, tile)]
    state = []
    for s in tiles:
        ur, ui = u_re[s, :], u_im[s, :]
        state.append((f_re * ur + f_im * ui, f_im * ur - f_re * ui))
    for sweep in range(ITERS):
        after = []
        for s, (yr, yi) in zip(tiles, state):
            pr, pi = coupled(yr, sweep), coupled(yi, sweep)
            ur, ui = u_re[s, :], u_im[s, :]
            top_re, top_im = f_re + pi, f_im - pr
            after.append((top_re * ur + top_im * ui, top_im * ur - top_re * ui))
        state = after
    for s, (yr, yi) in zip(tiles, state):
        w = jnp.concatenate([omega[s, :]] * (count // 128), 1)
        re, im = (yr * w).astype(bf16), (yi * w).astype(bf16)
        for_re[s, :count] = re
        for_re[s, count:] = -im
        for_im[s, :count] = im
        for_im[s, count:] = re


def solve(mine, other, prepared):
    total, count = prepared[0].shape
    operands = (mine, other, *prepared)
    shape = sds((total, 2 * count), bf16)
    return call(solve_body, [shape, shape], operands, specs=[VMEM] * 7, microseconds=4.0)


def peaks_tile(modes, for_re, for_im):
    total = for_im.shape[0]
    tile = 256
    best = jnp.zeros((8, modes.shape[1]), f32)
    for s in range(0, total, tile):
        re = mm(for_re[s : s + tile, :], modes)
        im = mm(for_im[s : s + tile, :], modes)
        square = re * re + im * im
        best = jnp.maximum(best, jnp.max(square.reshape(tile // 8, 8, modes.shape[1]), axis=0))
    return best


def parts_of(parts):
    at = 0
    for part in parts:
        for e in range(0, part.shape[1], BLOCK):
            yield at, part, e
            at += BLOCK


def half_peaks_body(for_re, for_im, far, middle_a, middle_b, near, best):
    for at, part, e in parts_of((far, middle_a, middle_b, near)):
        best[:, at : at + BLOCK] = peaks_tile(part[:, e : e + BLOCK], for_re, for_im)


def all_peaks_body(for_im, before, far, middle_a, middle_b, near, out, for_re):
    count = for_im.shape[1] // 2
    for_re[:, :count] = for_im[:, count:]
    for_re[:, count:] = -for_im[:, :count]
    rows = out.shape[1]
    end = far.shape[1]
    even = odd_core() == 0
    for at, part, e in parts_of((far, middle_a, middle_b, near)):
        best = jnp.maximum(before[:, at : at + BLOCK], peaks_tile(part[:, e : e + BLOCK], for_re, for_im))
        peak = jnp.sqrt(jnp.max(best, axis=0, keepdims=True))
        to = at
        if part is far:
            to = jnp.where(even, at, at + rows - end)
        if part is near:
            to = jnp.where(even, at, at - rows + end)
        out[0:1, pl.ds(pl.multiple_of(to, BLOCK), BLOCK)] = peak


def peaks(for_re, for_im, parts):
    total, twice = for_im.shape
    rows = sum(p.shape[1] for p in parts)
    there = lax.ppermute(for_im, "slab", CORE_PAIRS)
    best = call(half_peaks_body, [sds((8, rows), f32)], (for_re, for_im, *parts), microseconds=2.5)[0]
    out = call(
        all_peaks_body,
        [sds((1, rows), f32)],
        (there, best, *parts),
        [pltpu.VMEM((total, twice), bf16)],
        [VMEM] * 6,
        2.5,
    )[0]
    return out.reshape(rows)


def on_device(
    mode_shapes,
    unbalance,
    connectivity,
    stress_weights,
    face_low_nodes,
    face_high_nodes,
    natural_freq,
    damping_ratio,
    coupling,
    speed_index,
):
    rows, width = mode_shapes.shape
    reach = face_low_nodes.shape[0]
    low = face_low_nodes.reshape(1, reach)
    high = face_high_nodes.reshape(1, reach)

    speeds = speed_index.reshape(1, -1)
    force, shapes_t = first(unbalance, mode_shapes)
    small = sds((2, width // 2), f32)
    letter = sds((4, width // 2), f32)
    tables = pltpu.VMEM((2, WINDOW, BLOCK), bf16)
    table = pltpu.VMEM((rows, reach), bf16)

    def swap(x, number):
        return lax.ppermute(x, ("slab", "spd"), ROUNDS[number])

    def middle(blocks, force):
        return call(
            functools.partial(middle_body, blocks=blocks),
            [sds(force.shape, f32), sds((width, len(blocks) * BLOCK), bf16)],
            (force, connectivity, stress_weights, shapes_t),
            [tables],
            microseconds=MICRO * 1.2,
        )

    def end(halo, low_core, force):
        return call(
            functools.partial(end_body, low_core=low_core),
            [small, sds((width, 2 * BLOCK), bf16)],
            (force, connectivity, stress_weights, shapes_t, halo),
            [pltpu.VMEM((width, 3 * reach), bf16), tables],
            [VMEM] * 5,
            MICRO * 1.6,
        )

    arrived = lax.ppermute(force, "slab", CORE_PAIRS)
    force, middle_a = middle((2, 3), force)
    own = speeds.astype(f32)
    message = jnp.concatenate([force + arrived, own, own])
    arrived = swap(message, 0)
    message, far_rows = call(
        far_gather_body,
        [letter, sds((width, reach), bf16)],
        (message, low, high, shapes_t),
        [table],
        [VMEM] * 4,
        MICRO * 1.8,
    )
    far_halo = lax.ppermute(far_rows, ("slab", "spd"), FAR_PAIRS)
    message = jnp.concatenate([message[:2] + arrived[:2], message[2:3], arrived[2:3]])
    there = swap(message, 1)
    message, middle_b = middle((4, 5), message)
    force = message[:2] + there[:2]
    arrived, neighbour = swap(force, 2), arrived[2:3]
    force, near_rows = call(
        near_gather_body,
        [small, sds((width + 16, reach), bf16)],
        (force, neighbour, low, high, shapes_t),
        [table],
        [VMEM] * 5,
        MICRO * 1.8,
    )
    near_halo = lax.ppermute(near_rows, "slab", CORE_PAIRS)
    force = force + arrived
    arrived = swap(force, 3)
    force, far = end(far_halo, 0, force)
    force = force + arrived
    arrived = swap(force, 4)
    force, near = end(near_halo, 1, force)
    force, *prepared = prepare(force, speeds, there, near_halo, natural_freq, damping_ratio, coupling)
    force = force + arrived
    for_re, for_im = solve(force, lax.ppermute(force, "slab", CORE_PAIRS), prepared)
    return peaks(for_re, for_im, (far, middle_a, middle_b, near))


def solution(mesh):
    return jax.shard_map(
        on_device,
        mesh=mesh,
        in_specs=(
            P("slab", None),
            P(None, "slab"),
            P(None, "slab"),
            P(None, "slab"),
            P("slab"),
            P("slab"),
            P(),
            P(),
            P(),
            P("spd"),
        ),
        out_specs=P("slab"),
        check_vma=False,
    )
```

```python
import functools
import math

import jax
import jax.numpy as jnp
from jax import lax
from jax.experimental import pallas as pl
from jax.experimental.pallas import tpu as pltpu
from jax.sharding import PartitionSpec as P

ITERS = 6
EARLY = 4
NGRID = 4096
X, Y, Z, CORES = 4, 4, 8, 2
BLOCK = 256
WINDOW = 1280
CODE = 64
ROOM0 = 51
MICRO = 8.0
bf16 = jnp.bfloat16
f32 = jnp.float32


def mm(a, b):
    return jnp.dot(a, b, preferred_element_type=f32)


VMEM = pl.BlockSpec(memory_space=pltpu.VMEM)
HBM = pl.BlockSpec(memory_space=pltpu.HBM)


def call(body, out_shape, operands, scratch=(), specs=None, microseconds=1.0, room=24):
    return pl.pallas_call(
        body,
        out_shape=out_shape,
        in_specs=specs or [VMEM] * len(operands),
        out_specs=[VMEM] * len(out_shape),
        scratch_shapes=list(scratch),
        compiler_params=pltpu.CompilerParams(vmem_limit_bytes=int(room * 2**20)),
        cost_estimate=pl.CostEstimate(flops=int(1e9 * microseconds), bytes_accessed=0, transcendentals=0),
    )(*operands)


def sds(shape, dtype):
    return jax.ShapeDtypeStruct(shape, dtype)


def odd_core():
    return lax.rem(lax.axis_index("slab"), CORES)


def end_slab():
    slab = lax.axis_index("slab")
    return jnp.logical_or(slab == 0, slab == N_SLAB - 1)


def slab_of(x, z, c):
    return (x * Z + z) * CORES + c


def slab_pairs(partner):
    return [
        (slab_of(x, z, c), slab_of(*partner(x, z, c)))
        for x in range(X)
        for z in range(Z)
        for c in range(CORES)
    ]


CORE_PAIRS = slab_pairs(lambda x, z, c: (x, z, 1 - c))


def odd_round(partner, mirror=lambda y: y ^ 1):
    pairs = []
    for x in range(X):
        for z in range(Z):
            for y in range(Y):
                pairs.append((slab_of(x, z, 0) * Y + y, slab_of(x, z, 0) * Y + mirror(y)))
                pairs.append((slab_of(x, z, 1) * Y + y, slab_of(*partner(x, z), 1) * Y + y))
    return sorted(pairs)


ROUNDS = (
    odd_round(lambda x, z: (x ^ 1, z)),
    odd_round(lambda x, z: (3 - x, z), lambda y: 3 - y),
    odd_round(lambda x, z: (x, z ^ 1)),
    odd_round(lambda x, z: (x, z ^ 2)),
    odd_round(lambda x, z: (x, 7 - z)),
)
N_SLAB = X * Z * CORES
FAR_PAIRS = [
    (j * Y + y, (j + 1 if j % 2 else j - 1) * Y + y) if 0 < j < N_SLAB - 1 else (j * Y + y, j * Y + (y ^ 1))
    for j in range(N_SLAB)
    for y in range(Y)
]


def load_body(shapes, landing, sems):
    parts = sems.shape[0]
    step = shapes.shape[0] // parts
    copies = []
    for p in range(parts):
        s = pl.ds(p * step, step)
        copy = pltpu.make_async_copy(shapes.at[s, :], landing.at[s, :], sems.at[p])
        copy.start()
        copies.append(copy)
    for copy in copies:
        copy.wait()


def force_body(unbalance, shapes, force):
    total = mm(unbalance[...], shapes[...])
    half = total.shape[1] // 2
    force[0:1, :] = total[0:1, :half] - total[1:2, half:]
    force[1:2, :] = total[0:1, half:] + total[1:2, :half]


def turn_body(force_in, shapes, force_out, shapes_t):
    rows = shapes.shape[0]
    for r in range(0, rows, 2 * BLOCK):
        shapes_t[:, r : r + 2 * BLOCK] = jnp.transpose(shapes[r : r + 2 * BLOCK, :])
    force_out[...] = force_in[...]


def gather_rows(nodes, one, shapes_t, table):
    rows = shapes_t.shape[1]
    count = nodes.shape[1]
    here = jnp.broadcast_to(nodes.astype(jnp.int16), (16, count))
    row = lax.broadcasted_iota(jnp.int16, (16, count), 0)
    zero = jnp.zeros((16, count), bf16)
    for r in range(0, rows, 16):
        table[r : r + 16, :] = jnp.where(here == row + jnp.int16(r), one, zero)
    return mm(shapes_t[...], table[...]).astype(bf16)


def near_gather_body(message_in, speeds, low, high, shapes_t, message_out, out, table):
    width = shapes_t.shape[0]
    nodes = jnp.where(odd_core() == 0, high[...], low[...])
    one = jnp.ones((16, nodes.shape[1]), bf16)
    out[:width, :] = gather_rows(nodes, one, shapes_t, table)
    index = speeds[...].astype(jnp.int32)
    coarse = index // CODE
    fine = index - coarse * CODE
    row = jnp.concatenate([coarse.astype(f32), fine.astype(f32)], 1)
    out[width:, :] = jnp.broadcast_to(row, (16, row.shape[1])).astype(bf16)
    message_out[...] = message_in[...]


def far_gather_body(message_in, low, high, shapes_t, message_out, out, table):
    nodes = jnp.where(odd_core() == 0, low[...], high[...])
    one = jnp.full((16, nodes.shape[1]), jnp.where(end_slab(), 0.0, 1.0), f32).astype(bf16)
    out[...] = gather_rows(nodes, one, shapes_t, table)
    message_out[...] = message_in[...]


def fill_table(table, links, weights, start):
    corners, count = links.shape
    here = (links - start).astype(jnp.int16)
    here = [jnp.broadcast_to(here[k : k + 1, :], (16, count)) for k in range(corners)]
    value = [jnp.broadcast_to(weights[k : k + 1, :], (16, count)) for k in range(corners)]
    row = lax.broadcasted_iota(jnp.int16, (16, count), 0)
    for r in range(0, WINDOW, 16):
        at = row + jnp.int16(r)
        entry = jnp.zeros((16, count), bf16)
        for k in range(corners):
            entry = jnp.where(here[k] == at, value[k], entry)
        table[r : r + 16, :] = entry


def middle_body(force_in, links, weights, shapes_t, force_out, out, tables, *, blocks):
    for i, b in enumerate(blocks):
        s = slice(b * BLOCK, (b + 1) * BLOCK)
        fill_table(tables.at[i % 2], links[:, s], weights[:, s], b * BLOCK)
        start = (b - 2) * BLOCK
        modes = mm(shapes_t[:, start : start + WINDOW], tables[i % 2])
        out[:, i * BLOCK : (i + 1) * BLOCK] = modes.astype(bf16)
    force_out[...] = force_in[...]


def end_body(force_in, links, weights, shapes_t, halo, force_out, out, window, tables, *, low_core, inner):
    width, rows = shapes_t.shape
    reach = halo.shape[1]
    own = 1024

    low = odd_core() == low_core

    @pl.when(low)
    def _():
        window[:, :reach] = halo[:width, :]
        window[:, reach:] = shapes_t[:, :own]

    @pl.when(jnp.logical_not(low))
    def _():
        window[:, :own] = shapes_t[:, rows - own :]
        window[:, own:] = halo[:width, :]

    base = jnp.where(low, 0, rows - 2 * BLOCK)
    for i in range(2):
        start = pl.multiple_of(base + i * BLOCK, BLOCK)
        fill_table(tables.at[i], links[:, pl.ds(start, BLOCK)], weights[:, pl.ds(start, BLOCK)], start)
        modes = mm(window[:, i * BLOCK : i * BLOCK + WINDOW], tables[i])
        out[:, i * BLOCK : (i + 1) * BLOCK] = modes.astype(bf16)
    for i, b in enumerate(inner):
        s = slice(b * BLOCK, (b + 1) * BLOCK)
        fill_table(tables.at[i % 2], links[:, s], weights[:, s], b * BLOCK)
        modes = mm(shapes_t[:, (b - 2) * BLOCK : (b - 2) * BLOCK + WINDOW], tables[i % 2])
        out[:, (2 + i) * BLOCK : (3 + i) * BLOCK] = modes.astype(bf16)
    force_out[...] = force_in[...]


def split(x):
    high = x.astype(bf16)
    return high, (x - high.astype(f32)).astype(bf16)


def prepare_body(
    message_in, speeds, there, halo, freq, damping, coupling, message_out, u_re, u_im, omega_out, c_high, c_low
):
    count = freq.shape[1]
    total = u_re.shape[0]
    tail = halo[halo.shape[0] - 16 :, :].astype(f32)
    tail = tail[0:1, : total // 2] * CODE + tail[0:1, total // 2 :]
    odd = jnp.concatenate([speeds[...].astype(f32), tail], 1)
    even = jnp.concatenate([there[2:3, :], there[3:4, :]], 1)
    index = jnp.where(odd_core() == 0, even, odd)
    message_out[...] = message_in[...]
    omega = 0.25 + 4.0 * index / NGRID
    omega = jnp.transpose(jnp.broadcast_to(omega, (8, total)))[:, 0:1]
    omega = jnp.broadcast_to(omega, (total, count))
    f = freq[...]
    zeta = damping[...]
    d_re = f * f - omega * omega
    d_im = 2.0 * (zeta * f) * omega
    scale = omega / (d_re * d_re + d_im * d_im)
    u_re[...] = d_re * scale
    u_im[...] = d_im * scale
    omega_out[...] = omega[:, :128]
    i = lax.broadcasted_iota(jnp.int32, (count, count), 0)
    j = lax.broadcasted_iota(jnp.int32, (count, count), 1)
    coupled = jnp.transpose(coupling[...]) * (zeta * f * (1.5 / math.sqrt(count)))
    c_high[...], c_low[...] = split(jnp.where(i == j, 0.0, coupled))


def prepare(message, speeds, there, halo, freq, damping, coupling):
    total, count = 2 * speeds.shape[1], freq.shape[0]
    operands = (message, speeds, there, halo, freq.reshape(1, count), damping.reshape(1, count), coupling)
    return call(
        prepare_body,
        [
            sds(message.shape, f32),
            sds((total, count), f32),
            sds((total, count), f32),
            sds((total, 128), f32),
            sds((count, count), bf16),
            sds((count, count), bf16),
        ],
        operands,
        specs=[VMEM] * 7,
        microseconds=0.9,
    )


def solve_body(mine, other, u_re, u_im, omega, c_high, c_low, for_re, for_im):
    force = jnp.where(odd_core() == 1, mine[...], other[...])
    f_re, f_im = force[0:1, :], force[1:2, :]
    ch, cl = c_high[...], c_low[...]

    def coupled(y, sweep):
        if sweep < EARLY:
            return mm(y.astype(bf16), ch)
        high, low = split(y)
        return mm(high, ch) + (mm(low, ch) + mm(high, cl))

    total, count = u_re.shape
    tile = 256
    tiles = [pl.ds(t, tile) for t in range(0, total, tile)]
    state = []
    for s in tiles:
        ur, ui = u_re[s, :], u_im[s, :]
        state.append((f_re * ur + f_im * ui, f_im * ur - f_re * ui))
    for sweep in range(ITERS):
        after = []
        for s, (yr, yi) in zip(tiles, state):
            pr, pi = coupled(yr, sweep), coupled(yi, sweep)
            ur, ui = u_re[s, :], u_im[s, :]
            top_re, top_im = f_re + pi, f_im - pr
            after.append((top_re * ur + top_im * ui, top_im * ur - top_re * ui))
        state = after
    for s, (yr, yi) in zip(tiles, state):
        w = jnp.concatenate([omega[s, :]] * (count // 128), 1)
        re, im = (yr * w).astype(bf16), (yi * w).astype(bf16)
        for_re[s, :count] = re
        for_re[s, count:] = -im
        for_im[s, :count] = im
        for_im[s, count:] = re


def solve(mine, other, prepared):
    total, count = prepared[0].shape
    operands = (mine, other, *prepared)
    shape = sds((total, 2 * count), bf16)
    return call(solve_body, [shape, shape], operands, specs=[VMEM] * 7, microseconds=4.0)


def peaks_tile(modes, for_re, for_im):
    total = for_im.shape[0]
    tile = 256
    best = jnp.zeros((8, modes.shape[1]), f32)
    for s in range(0, total, tile):
        re = mm(for_re[s : s + tile, :], modes)
        im = mm(for_im[s : s + tile, :], modes)
        square = re * re + im * im
        best = jnp.maximum(best, jnp.max(square.reshape(tile // 8, 8, modes.shape[1]), axis=0))
    return best


def parts_of(parts):
    at = 0
    for part in parts:
        for e in range(0, part.shape[1], BLOCK):
            yield at, part, e
            at += BLOCK


def half_peaks_body(for_re, for_im, far, middle, near, best):
    for at, part, e in parts_of((far, middle, near)):
        best[:, at : at + BLOCK] = peaks_tile(part[:, e : e + BLOCK], for_re, for_im)


def all_peaks_body(for_im, before, far, middle, near, out, for_re):
    count = for_im.shape[1] // 2
    for_re[:, :count] = for_im[:, count:]
    for_re[:, count:] = -for_im[:, :count]
    rows = out.shape[1]
    even = odd_core() == 0
    for at, part, e in parts_of((far, middle, near)):
        best = jnp.maximum(before[:, at : at + BLOCK], peaks_tile(part[:, e : e + BLOCK], for_re, for_im))
        peak = jnp.sqrt(jnp.max(best, axis=0, keepdims=True))
        first, last = e, rows - 2 * BLOCK + e
        if part is middle:
            to = 2 * BLOCK + e
        elif part is near:
            to = jnp.where(even, last, first)
        elif e < 2 * BLOCK:
            to = jnp.where(even, first, last)
        else:
            to = 5 * BLOCK
        out[0:1, pl.ds(pl.multiple_of(to, BLOCK), BLOCK)] = peak


def peaks(for_re, for_im, parts):
    total, twice = for_im.shape
    rows = sum(p.shape[1] for p in parts)
    there = lax.ppermute(for_im, "slab", CORE_PAIRS)
    best = call(half_peaks_body, [sds((8, rows), f32)], (for_re, for_im, *parts), microseconds=2.5)[0]
    out = call(
        all_peaks_body,
        [sds((1, rows), f32)],
        (there, best, *parts),
        [pltpu.VMEM((total, twice), bf16)],
        [VMEM] * 5,
        2.5,
    )[0]
    return out.reshape(rows)


def on_device(
    mode_shapes,
    unbalance,
    connectivity,
    stress_weights,
    face_low_nodes,
    face_high_nodes,
    natural_freq,
    damping_ratio,
    coupling,
    speed_index,
):
    rows, width = mode_shapes.shape
    reach = face_low_nodes.shape[0]
    low = face_low_nodes.reshape(1, reach)
    high = face_high_nodes.reshape(1, reach)

    speeds = speed_index.reshape(1, -1)
    shapes = call(
        load_body,
        [sds((rows, width), bf16)],
        (mode_shapes,),
        [pltpu.SemaphoreType.DMA((4,))],
        [HBM],
        1.5,
        ROOM0,
    )[0]
    force = call(force_body, [sds((2, width // 2), f32)], (unbalance, shapes), microseconds=0.5)[0]
    small = sds((2, width // 2), f32)
    letter = sds((4, width // 2), f32)
    tables = pltpu.VMEM((2, WINDOW, BLOCK), bf16)
    table = pltpu.VMEM((rows, reach), bf16)

    def swap(x, number):
        return lax.ppermute(x, ("slab", "spd"), ROUNDS[number])

    def middle(blocks, force):
        return call(
            functools.partial(middle_body, blocks=blocks),
            [sds(force.shape, f32), sds((width, len(blocks) * BLOCK), bf16)],
            (force, connectivity, stress_weights, shapes_t),
            [tables],
            microseconds=MICRO * 2.2,
        )

    def end(halo, low_core, inner, force):
        return call(
            functools.partial(end_body, low_core=low_core, inner=inner),
            [small, sds((width, (2 + len(inner)) * BLOCK), bf16)],
            (force, connectivity, stress_weights, shapes_t, halo),
            [pltpu.VMEM((width, 3 * reach), bf16), tables],
            [VMEM] * 5,
            MICRO * 1.6,
        )

    arrived = lax.ppermute(force, "slab", CORE_PAIRS)
    force, shapes_t = call(
        turn_body, [small, sds((width, rows), bf16)], (force, shapes), microseconds=MICRO * 0.6
    )
    own = speeds.astype(f32)
    message = jnp.concatenate([force + arrived, own, own])
    arrived = swap(message, 0)
    message, far_rows = call(
        far_gather_body,
        [letter, sds((width, reach), bf16)],
        (message, low, high, shapes_t),
        [table],
        [VMEM] * 4,
        MICRO * 1.8,
    )
    far_halo = lax.ppermute(far_rows, ("slab", "spd"), FAR_PAIRS)
    message = jnp.concatenate([message[:2] + arrived[:2], message[2:3], arrived[2:3]])
    there = swap(message, 1)
    message, central = middle((2, 3, 4), message)
    force = message[:2] + there[:2]
    arrived, neighbour = swap(force, 2), arrived[2:3]
    force, near_rows = call(
        near_gather_body,
        [small, sds((width + 16, reach), bf16)],
        (force, neighbour, low, high, shapes_t),
        [table],
        [VMEM] * 5,
        MICRO * 1.8,
    )
    near_halo = lax.ppermute(near_rows, "slab", CORE_PAIRS)
    force = force + arrived
    arrived = swap(force, 3)
    force, far = end(far_halo, 0, (5,), force)
    force = force + arrived
    arrived = swap(force, 4)
    force, near = end(near_halo, 1, (), force)
    force, *prepared = prepare(force, speeds, there, near_halo, natural_freq, damping_ratio, coupling)
    force = force + arrived
    for_re, for_im = solve(force, lax.ppermute(force, "slab", CORE_PAIRS), prepared)
    return peaks(for_re, for_im, (far, central, near))


def solution(mesh):
    return jax.shard_map(
        on_device,
        mesh=mesh,
        in_specs=(
            P("slab", None),
            P(None, "slab"),
            P(None, "slab"),
            P(None, "slab"),
            P("slab"),
            P("slab"),
            P(),
            P(),
            P(),
            P("spd"),
        ),
        out_specs=P("slab"),
        check_vma=False,
    )
```

```python
import functools
import math

import jax
import jax.numpy as jnp
from jax import lax
from jax.experimental import pallas as pl
from jax.experimental.pallas import tpu as pltpu
from jax.sharding import PartitionSpec as P

ITERS = 6
EARLY = 4
NGRID = 4096
X, Y, Z, CORES = 4, 4, 8, 2
BLOCK = 256
WINDOW = 1280
CODE = 64
ROOM0 = 51
MICRO = 8.0
bf16 = jnp.bfloat16
f32 = jnp.float32


def mm(a, b):
    return jnp.dot(a, b, preferred_element_type=f32)


VMEM = pl.BlockSpec(memory_space=pltpu.VMEM)
HBM = pl.BlockSpec(memory_space=pltpu.HBM)


def call(body, out_shape, operands, scratch=(), specs=None, microseconds=1.0, room=24):
    return pl.pallas_call(
        body,
        out_shape=out_shape,
        in_specs=specs or [VMEM] * len(operands),
        out_specs=[VMEM] * len(out_shape),
        scratch_shapes=list(scratch),
        compiler_params=pltpu.CompilerParams(vmem_limit_bytes=int(room * 2**20)),
        cost_estimate=pl.CostEstimate(flops=int(1e9 * microseconds), bytes_accessed=0, transcendentals=0),
    )(*operands)


def sds(shape, dtype):
    return jax.ShapeDtypeStruct(shape, dtype)


def odd_core():
    return lax.rem(lax.axis_index("slab"), CORES)


def end_slab():
    slab = lax.axis_index("slab")
    return jnp.logical_or(slab == 0, slab == N_SLAB - 1)


def slab_of(x, z, c):
    return (x * Z + z) * CORES + c


def slab_pairs(partner):
    return [
        (slab_of(x, z, c), slab_of(*partner(x, z, c)))
        for x in range(X)
        for z in range(Z)
        for c in range(CORES)
    ]


CORE_PAIRS = slab_pairs(lambda x, z, c: (x, z, 1 - c))


def near_row(x, z, y):
    return y ^ 1


def mirror_row(x, z, y):
    return Y - 1 - y


def patient(x, z):
    return z == 0 and x > 0


def odd_round(partner, row=near_row):
    pairs = []
    for x in range(X):
        for z in range(Z):
            for y in range(Y):
                pairs.append((slab_of(x, z, 0) * Y + y, slab_of(x, z, 0) * Y + row(x, z, y)))
                pairs.append((slab_of(x, z, 1) * Y + y, slab_of(*partner(x, z), 1) * Y + y))
    return sorted(pairs)


ROUNDS = (
    odd_round(lambda x, z: (x ^ 1, z), lambda x, z, y: (mirror_row if patient(x, z) else near_row)(x, z, y)),
    odd_round(lambda x, z: (3 - x, z), lambda x, z, y: (near_row if patient(x, z) else mirror_row)(x, z, y)),
    odd_round(lambda x, z: (x, z ^ 1)),
    odd_round(lambda x, z: (x, z ^ 2)),
    odd_round(lambda x, z: (x, 7 - z)),
)
N_SLAB = X * Z * CORES
FAR_PAIRS = [
    (j * Y + y, (j + 1 if j % 2 else j - 1) * Y + y) if 0 < j < N_SLAB - 1 else (j * Y + y, j * Y + (y ^ 1))
    for j in range(N_SLAB)
    for y in range(Y)
]


def load_body(shapes, landing, sems):
    parts = sems.shape[0]
    step = shapes.shape[0] // parts
    copies = []
    for p in range(parts):
        s = pl.ds(p * step, step)
        copy = pltpu.make_async_copy(shapes.at[s, :], landing.at[s, :], sems.at[p])
        copy.start()
        copies.append(copy)
    for copy in copies:
        copy.wait()


def force_body(unbalance, shapes, force):
    total = mm(unbalance[...], shapes[...])
    half = total.shape[1] // 2
    force[0:1, :] = total[0:1, :half] - total[1:2, half:]
    force[1:2, :] = total[0:1, half:] + total[1:2, :half]


def turn_body(force_in, shapes, force_out, shapes_t):
    rows = shapes.shape[0]
    for r in range(0, rows, 2 * BLOCK):
        shapes_t[:, r : r + 2 * BLOCK] = jnp.transpose(shapes[r : r + 2 * BLOCK, :])
    force_out[...] = force_in[...]


def gather_rows(nodes, one, shapes_t, table):
    rows = shapes_t.shape[1]
    count = nodes.shape[1]
    here = jnp.broadcast_to(nodes.astype(jnp.int16), (16, count))
    row = lax.broadcasted_iota(jnp.int16, (16, count), 0)
    zero = jnp.zeros((16, count), bf16)
    for r in range(0, rows, 16):
        table[r : r + 16, :] = jnp.where(here == row + jnp.int16(r), one, zero)
    return mm(shapes_t[...], table[...]).astype(bf16)


def near_gather_body(message_in, speeds, low, high, shapes_t, message_out, out, table):
    width = shapes_t.shape[0]
    nodes = jnp.where(odd_core() == 0, high[...], low[...])
    one = jnp.ones((16, nodes.shape[1]), bf16)
    out[:width, :] = gather_rows(nodes, one, shapes_t, table)
    index = speeds[...].astype(jnp.int32)
    coarse = index // CODE
    fine = index - coarse * CODE
    row = jnp.concatenate([coarse.astype(f32), fine.astype(f32)], 1)
    out[width:, :] = jnp.broadcast_to(row, (16, row.shape[1])).astype(bf16)
    message_out[...] = message_in[...]


def far_gather_body(message_in, low, high, shapes_t, message_out, out, table):
    nodes = jnp.where(odd_core() == 0, low[...], high[...])
    one = jnp.full((16, nodes.shape[1]), jnp.where(end_slab(), 0.0, 1.0), f32).astype(bf16)
    out[...] = gather_rows(nodes, one, shapes_t, table)
    message_out[...] = message_in[...]


def fill_table(table, links, weights, start):
    corners, count = links.shape
    here = (links - start).astype(jnp.int16)
    here = [jnp.broadcast_to(here[k : k + 1, :], (16, count)) for k in range(corners)]
    value = [jnp.broadcast_to(weights[k : k + 1, :], (16, count)) for k in range(corners)]
    row = lax.broadcasted_iota(jnp.int16, (16, count), 0)
    for r in range(0, WINDOW, 16):
        at = row + jnp.int16(r)
        entry = jnp.zeros((16, count), bf16)
        for k in range(corners):
            entry = jnp.where(here[k] == at, value[k], entry)
        table[r : r + 16, :] = entry


def middle_body(force_in, links, weights, shapes_t, force_out, out, tables, *, blocks):
    for i, b in enumerate(blocks):
        s = slice(b * BLOCK, (b + 1) * BLOCK)
        fill_table(tables.at[i % 2], links[:, s], weights[:, s], b * BLOCK)
        start = (b - 2) * BLOCK
        modes = mm(shapes_t[:, start : start + WINDOW], tables[i % 2])
        out[:, i * BLOCK : (i + 1) * BLOCK] = modes.astype(bf16)
    force_out[...] = force_in[...]


def end_body(force_in, links, weights, shapes_t, halo, force_out, out, window, tables, *, low_core, inner):
    width, rows = shapes_t.shape
    reach = halo.shape[1]
    own = 1024

    low = odd_core() == low_core

    @pl.when(low)
    def _():
        window[:, :reach] = halo[:width, :]
        window[:, reach:] = shapes_t[:, :own]

    @pl.when(jnp.logical_not(low))
    def _():
        window[:, :own] = shapes_t[:, rows - own :]
        window[:, own:] = halo[:width, :]

    base = jnp.where(low, 0, rows - 2 * BLOCK)
    for i in range(2):
        start = pl.multiple_of(base + i * BLOCK, BLOCK)
        fill_table(tables.at[i], links[:, pl.ds(start, BLOCK)], weights[:, pl.ds(start, BLOCK)], start)
        modes = mm(window[:, i * BLOCK : i * BLOCK + WINDOW], tables[i])
        out[:, i * BLOCK : (i + 1) * BLOCK] = modes.astype(bf16)
    for i, b in enumerate(inner):
        s = slice(b * BLOCK, (b + 1) * BLOCK)
        fill_table(tables.at[i % 2], links[:, s], weights[:, s], b * BLOCK)
        modes = mm(shapes_t[:, (b - 2) * BLOCK : (b - 2) * BLOCK + WINDOW], tables[i % 2])
        out[:, (2 + i) * BLOCK : (3 + i) * BLOCK] = modes.astype(bf16)
    force_out[...] = force_in[...]


def split(x):
    high = x.astype(bf16)
    return high, (x - high.astype(f32)).astype(bf16)


def prepare_body(
    message_in, speeds, there, halo, freq, damping, coupling, message_out, u_re, u_im, omega_out, c_high, c_low
):
    count = freq.shape[1]
    total = u_re.shape[0]
    tail = halo[halo.shape[0] - 16 :, :].astype(f32)
    tail = tail[0:1, : total // 2] * CODE + tail[0:1, total // 2 :]
    odd = jnp.concatenate([speeds[...].astype(f32), tail], 1)
    even = jnp.concatenate([there[2:3, :], there[3:4, :]], 1)
    index = jnp.where(odd_core() == 0, even, odd)
    message_out[...] = message_in[...]
    omega = 0.25 + 4.0 * index / NGRID
    omega = jnp.transpose(jnp.broadcast_to(omega, (8, total)))[:, 0:1]
    omega = jnp.broadcast_to(omega, (total, count))
    f = freq[...]
    zeta = damping[...]
    d_re = f * f - omega * omega
    d_im = 2.0 * (zeta * f) * omega
    scale = omega / (d_re * d_re + d_im * d_im)
    u_re[...] = d_re * scale
    u_im[...] = d_im * scale
    omega_out[...] = omega[:, :128]
    i = lax.broadcasted_iota(jnp.int32, (count, count), 0)
    j = lax.broadcasted_iota(jnp.int32, (count, count), 1)
    coupled = jnp.transpose(coupling[...]) * (zeta * f * (1.5 / math.sqrt(count)))
    c_high[...], c_low[...] = split(jnp.where(i == j, 0.0, coupled))


def prepare(message, speeds, there, halo, freq, damping, coupling):
    total, count = 2 * speeds.shape[1], freq.shape[0]
    operands = (message, speeds, there, halo, freq.reshape(1, count), damping.reshape(1, count), coupling)
    return call(
        prepare_body,
        [
            sds(message.shape, f32),
            sds((total, count), f32),
            sds((total, count), f32),
            sds((total, 128), f32),
            sds((count, count), bf16),
            sds((count, count), bf16),
        ],
        operands,
        specs=[VMEM] * 7,
        microseconds=0.9,
    )


def solve_body(mine, other, u_re, u_im, omega, c_high, c_low, for_re, for_im):
    force = jnp.where(odd_core() == 1, mine[...], other[...])
    f_re, f_im = force[0:1, :], force[1:2, :]
    ch, cl = c_high[...], c_low[...]

    def coupled(y, sweep):
        if sweep < EARLY:
            return mm(y.astype(bf16), ch)
        high, low = split(y)
        return mm(high, ch) + (mm(low, ch) + mm(high, cl))

    total, count = u_re.shape
    tile = 256
    tiles = [pl.ds(t, tile) for t in range(0, total, tile)]
    state = []
    for s in tiles:
        ur, ui = u_re[s, :], u_im[s, :]
        state.append((f_re * ur + f_im * ui, f_im * ur - f_re * ui))
    for sweep in range(ITERS):
        after = []
        for s, (yr, yi) in zip(tiles, state):
            pr, pi = coupled(yr, sweep), coupled(yi, sweep)
            ur, ui = u_re[s, :], u_im[s, :]
            top_re, top_im = f_re + pi, f_im - pr
            after.append((top_re * ur + top_im * ui, top_im * ur - top_re * ui))
        state = after
    for s, (yr, yi) in zip(tiles, state):
        w = jnp.concatenate([omega[s, :]] * (count // 128), 1)
        re, im = (yr * w).astype(bf16), (yi * w).astype(bf16)
        for_re[s, :count] = re
        for_re[s, count:] = -im
        for_im[s, :count] = im
        for_im[s, count:] = re


def solve(mine, other, prepared):
    total, count = prepared[0].shape
    operands = (mine, other, *prepared)
    shape = sds((total, 2 * count), bf16)
    return call(solve_body, [shape, shape], operands, specs=[VMEM] * 7, microseconds=4.0)


def peaks_tile(modes, for_re, for_im):
    total = for_im.shape[0]
    tile = 256
    best = jnp.zeros((8, modes.shape[1]), f32)
    for s in range(0, total, tile):
        re = mm(for_re[s : s + tile, :], modes)
        im = mm(for_im[s : s + tile, :], modes)
        square = re * re + im * im
        best = jnp.maximum(best, jnp.max(square.reshape(tile // 8, 8, modes.shape[1]), axis=0))
    return best


def parts_of(parts):
    at = 0
    for part in parts:
        for e in range(0, part.shape[1], BLOCK):
            yield at, part, e
            at += BLOCK


def half_peaks_body(for_re, for_im, far, middle, near, best):
    for at, part, e in parts_of((far, middle, near)):
        best[:, at : at + BLOCK] = peaks_tile(part[:, e : e + BLOCK], for_re, for_im)


def all_peaks_body(for_im, before, far, middle, near, out, for_re):
    count = for_im.shape[1] // 2
    for_re[:, :count] = for_im[:, count:]
    for_re[:, count:] = -for_im[:, :count]
    rows = out.shape[1]
    even = odd_core() == 0
    for at, part, e in parts_of((far, middle, near)):
        best = jnp.maximum(before[:, at : at + BLOCK], peaks_tile(part[:, e : e + BLOCK], for_re, for_im))
        peak = jnp.sqrt(jnp.max(best, axis=0, keepdims=True))
        first, last = e, rows - 2 * BLOCK + e
        if part is middle:
            to = 2 * BLOCK + e
        elif part is near:
            to = jnp.where(even, last, first)
        elif e < 2 * BLOCK:
            to = jnp.where(even, first, last)
        else:
            to = 5 * BLOCK
        out[0:1, pl.ds(pl.multiple_of(to, BLOCK), BLOCK)] = peak


def peaks(for_re, for_im, parts):
    total, twice = for_im.shape
    rows = sum(p.shape[1] for p in parts)
    there = lax.ppermute(for_im, "slab", CORE_PAIRS)
    best = call(half_peaks_body, [sds((8, rows), f32)], (for_re, for_im, *parts), microseconds=2.5)[0]
    out = call(
        all_peaks_body,
        [sds((1, rows), f32)],
        (there, best, *parts),
        [pltpu.VMEM((total, twice), bf16)],
        [VMEM] * 5,
        2.5,
    )[0]
    return out.reshape(rows)


def on_device(
    mode_shapes,
    unbalance,
    connectivity,
    stress_weights,
    face_low_nodes,
    face_high_nodes,
    natural_freq,
    damping_ratio,
    coupling,
    speed_index,
):
    rows, width = mode_shapes.shape
    reach = face_low_nodes.shape[0]
    low = face_low_nodes.reshape(1, reach)
    high = face_high_nodes.reshape(1, reach)

    speeds = speed_index.reshape(1, -1)
    shapes = call(
        load_body,
        [sds((rows, width), bf16)],
        (mode_shapes,),
        [pltpu.SemaphoreType.DMA((4,))],
        [HBM],
        1.5,
        ROOM0,
    )[0]
    force = call(force_body, [sds((2, width // 2), f32)], (unbalance, shapes), microseconds=0.5)[0]
    small = sds((2, width // 2), f32)
    letter = sds((4, width // 2), f32)
    tables = pltpu.VMEM((2, WINDOW, BLOCK), bf16)
    table = pltpu.VMEM((rows, reach), bf16)

    def swap(x, number):
        return lax.ppermute(x, ("slab", "spd"), ROUNDS[number])

    def middle(blocks, force):
        return call(
            functools.partial(middle_body, blocks=blocks),
            [sds(force.shape, f32), sds((width, len(blocks) * BLOCK), bf16)],
            (force, connectivity, stress_weights, shapes_t),
            [tables],
            microseconds=MICRO * 2.2,
        )

    def end(halo, low_core, inner, force):
        return call(
            functools.partial(end_body, low_core=low_core, inner=inner),
            [small, sds((width, (2 + len(inner)) * BLOCK), bf16)],
            (force, connectivity, stress_weights, shapes_t, halo),
            [pltpu.VMEM((width, 3 * reach), bf16), tables],
            [VMEM] * 5,
            MICRO * 1.6,
        )

    arrived = lax.ppermute(force, "slab", CORE_PAIRS)
    force, shapes_t = call(
        turn_body, [small, sds((width, rows), bf16)], (force, shapes), microseconds=MICRO * 0.6
    )
    own = speeds.astype(f32)
    message = jnp.concatenate([force + arrived, own, own])
    arrived = swap(message, 0)
    message, far_rows = call(
        far_gather_body,
        [letter, sds((width, reach), bf16)],
        (message, low, high, shapes_t),
        [table],
        [VMEM] * 4,
        MICRO * 1.8,
    )
    far_halo = lax.ppermute(far_rows, ("slab", "spd"), FAR_PAIRS)
    message = jnp.concatenate([message[:2] + arrived[:2], message[2:3], arrived[2:3]])
    there = swap(message, 1)
    message, central = middle((2, 3, 4), message)
    force = message[:2] + there[:2]
    arrived, neighbour = swap(force, 2), arrived[2:3]
    force, near_rows = call(
        near_gather_body,
        [small, sds((width + 16, reach), bf16)],
        (force, neighbour, low, high, shapes_t),
        [table],
        [VMEM] * 5,
        MICRO * 1.8,
    )
    near_halo = lax.ppermute(near_rows, "slab", CORE_PAIRS)
    force = force + arrived
    arrived = swap(force, 3)
    force, far = end(far_halo, 0, (5,), force)
    force = force + arrived
    arrived = swap(force, 4)
    force, near = end(near_halo, 1, (), force)
    force, *prepared = prepare(force, speeds, there, near_halo, natural_freq, damping_ratio, coupling)
    force = force + arrived
    for_re, for_im = solve(force, lax.ppermute(force, "slab", CORE_PAIRS), prepared)
    return peaks(for_re, for_im, (far, central, near))


def solution(mesh):
    return jax.shard_map(
        on_device,
        mesh=mesh,
        in_specs=(
            P("slab", None),
            P(None, "slab"),
            P(None, "slab"),
            P(None, "slab"),
            P("slab"),
            P("slab"),
            P(),
            P(),
            P(),
            P("spd"),
        ),
        out_specs=P("slab"),
        check_vma=False,
    )
```

```python
import functools
import math

import jax
import jax.numpy as jnp
from jax import lax
from jax.experimental import pallas as pl
from jax.experimental.pallas import tpu as pltpu
from jax.sharding import PartitionSpec as P

ITERS = 6
EARLY = 5
NGRID = 4096
X, Y, Z, CORES = 4, 4, 8, 2
BLOCK = 256
WINDOW = 1280
CODE = 64
ROOM0 = 51
MICRO = 8.0
bf16 = jnp.bfloat16
f32 = jnp.float32


def mm(a, b):
    return jnp.dot(a, b, preferred_element_type=f32)


VMEM = pl.BlockSpec(memory_space=pltpu.VMEM)
HBM = pl.BlockSpec(memory_space=pltpu.HBM)


def call(body, out_shape, operands, scratch=(), specs=None, microseconds=1.0, room=24):
    return pl.pallas_call(
        body,
        out_shape=out_shape,
        in_specs=specs or [VMEM] * len(operands),
        out_specs=[VMEM] * len(out_shape),
        scratch_shapes=list(scratch),
        compiler_params=pltpu.CompilerParams(vmem_limit_bytes=int(room * 2**20)),
        cost_estimate=pl.CostEstimate(flops=int(1e9 * microseconds), bytes_accessed=0, transcendentals=0),
    )(*operands)


def sds(shape, dtype):
    return jax.ShapeDtypeStruct(shape, dtype)


def odd_core():
    return lax.rem(lax.axis_index("slab"), CORES)


def end_slab():
    slab = lax.axis_index("slab")
    return jnp.logical_or(slab == 0, slab == N_SLAB - 1)


def slab_of(x, z, c):
    return (x * Z + z) * CORES + c


def slab_pairs(partner):
    return [
        (slab_of(x, z, c), slab_of(*partner(x, z, c)))
        for x in range(X)
        for z in range(Z)
        for c in range(CORES)
    ]


CORE_PAIRS = slab_pairs(lambda x, z, c: (x, z, 1 - c))


def near_row(x, z, y):
    return y ^ 1


def mirror_row(x, z, y):
    return Y - 1 - y


def patient(x, z):
    return z == 0 and x > 0


def odd_round(partner, row=near_row):
    pairs = []
    for x in range(X):
        for z in range(Z):
            for y in range(Y):
                pairs.append((slab_of(x, z, 0) * Y + y, slab_of(x, z, 0) * Y + row(x, z, y)))
                pairs.append((slab_of(x, z, 1) * Y + y, slab_of(*partner(x, z), 1) * Y + y))
    return sorted(pairs)


ROUNDS = (
    odd_round(lambda x, z: (x ^ 1, z), lambda x, z, y: (mirror_row if patient(x, z) else near_row)(x, z, y)),
    odd_round(lambda x, z: (3 - x, z), lambda x, z, y: (near_row if patient(x, z) else mirror_row)(x, z, y)),
    odd_round(lambda x, z: (x, z ^ 1)),
    odd_round(lambda x, z: (x, z ^ 2)),
    odd_round(lambda x, z: (x, 7 - z)),
)
N_SLAB = X * Z * CORES
FAR_PAIRS = [
    (j * Y + y, (j + 1 if j % 2 else j - 1) * Y + y) if 0 < j < N_SLAB - 1 else (j * Y + y, j * Y + (y ^ 1))
    for j in range(N_SLAB)
    for y in range(Y)
]


def load_body(shapes, landing, sems):
    parts = sems.shape[0]
    step = shapes.shape[0] // parts
    copies = []
    for p in range(parts):
        s = pl.ds(p * step, step)
        copy = pltpu.make_async_copy(shapes.at[s, :], landing.at[s, :], sems.at[p])
        copy.start()
        copies.append(copy)
    for copy in copies:
        copy.wait()


def force_body(unbalance, shapes, force):
    total = mm(unbalance[...], shapes[...])
    half = total.shape[1] // 2
    force[0:1, :] = total[0:1, :half] - total[1:2, half:]
    force[1:2, :] = total[0:1, half:] + total[1:2, :half]


def turn_body(force_in, shapes, force_out, shapes_t):
    rows = shapes.shape[0]
    for r in range(0, rows, 2 * BLOCK):
        shapes_t[:, r : r + 2 * BLOCK] = jnp.transpose(shapes[r : r + 2 * BLOCK, :])
    force_out[...] = force_in[...]


def gather_rows(nodes, one, shapes_t, table):
    rows = shapes_t.shape[1]
    count = nodes.shape[1]
    here = jnp.broadcast_to(nodes.astype(jnp.int16), (16, count))
    row = lax.broadcasted_iota(jnp.int16, (16, count), 0)
    zero = jnp.zeros((16, count), bf16)
    for r in range(0, rows, 16):
        table[r : r + 16, :] = jnp.where(here == row + jnp.int16(r), one, zero)
    return mm(shapes_t[...], table[...]).astype(bf16)


def near_gather_body(message_in, speeds, low, high, shapes_t, message_out, out, table):
    width = shapes_t.shape[0]
    nodes = jnp.where(odd_core() == 0, high[...], low[...])
    one = jnp.ones((16, nodes.shape[1]), bf16)
    out[:width, :] = gather_rows(nodes, one, shapes_t, table)
    index = speeds[...].astype(jnp.int32)
    coarse = index // CODE
    fine = index - coarse * CODE
    row = jnp.concatenate([coarse.astype(f32), fine.astype(f32)], 1)
    out[width:, :] = jnp.broadcast_to(row, (16, row.shape[1])).astype(bf16)
    message_out[...] = message_in[...]


def far_gather_body(message_in, low, high, shapes_t, message_out, out, table):
    nodes = jnp.where(odd_core() == 0, low[...], high[...])
    one = jnp.full((16, nodes.shape[1]), jnp.where(end_slab(), 0.0, 1.0), f32).astype(bf16)
    out[...] = gather_rows(nodes, one, shapes_t, table)
    message_out[...] = message_in[...]


def fill_table(table, links, weights, start):
    corners, count = links.shape
    here = (links - start).astype(jnp.int16)
    here = [jnp.broadcast_to(here[k : k + 1, :], (16, count)) for k in range(corners)]
    value = [jnp.broadcast_to(weights[k : k + 1, :], (16, count)) for k in range(corners)]
    row = lax.broadcasted_iota(jnp.int16, (16, count), 0)
    for r in range(0, WINDOW, 16):
        at = row + jnp.int16(r)
        entry = jnp.zeros((16, count), bf16)
        for k in range(corners):
            entry = jnp.where(here[k] == at, value[k], entry)
        table[r : r + 16, :] = entry


def middle_body(force_in, links, weights, shapes_t, force_out, out, tables, *, blocks):
    for i, b in enumerate(blocks):
        s = slice(b * BLOCK, (b + 1) * BLOCK)
        fill_table(tables.at[i % 2], links[:, s], weights[:, s], b * BLOCK)
        start = (b - 2) * BLOCK
        modes = mm(shapes_t[:, start : start + WINDOW], tables[i % 2])
        out[:, i * BLOCK : (i + 1) * BLOCK] = modes.astype(bf16)
    force_out[...] = force_in[...]


def end_body(force_in, links, weights, shapes_t, halo, force_out, out, window, tables, *, low_core, inner):
    width, rows = shapes_t.shape
    reach = halo.shape[1]
    own = 1024

    low = odd_core() == low_core

    @pl.when(low)
    def _():
        window[:, :reach] = halo[:width, :]
        window[:, reach:] = shapes_t[:, :own]

    @pl.when(jnp.logical_not(low))
    def _():
        window[:, :own] = shapes_t[:, rows - own :]
        window[:, own:] = halo[:width, :]

    base = jnp.where(low, 0, rows - 2 * BLOCK)
    for i in range(2):
        start = pl.multiple_of(base + i * BLOCK, BLOCK)
        fill_table(tables.at[i], links[:, pl.ds(start, BLOCK)], weights[:, pl.ds(start, BLOCK)], start)
        modes = mm(window[:, i * BLOCK : i * BLOCK + WINDOW], tables[i])
        out[:, i * BLOCK : (i + 1) * BLOCK] = modes.astype(bf16)
    for i, b in enumerate(inner):
        s = slice(b * BLOCK, (b + 1) * BLOCK)
        fill_table(tables.at[i % 2], links[:, s], weights[:, s], b * BLOCK)
        modes = mm(shapes_t[:, (b - 2) * BLOCK : (b - 2) * BLOCK + WINDOW], tables[i % 2])
        out[:, (2 + i) * BLOCK : (3 + i) * BLOCK] = modes.astype(bf16)
    force_out[...] = force_in[...]


def split(x):
    high = x.astype(bf16)
    return high, (x - high.astype(f32)).astype(bf16)


def prepare_body(
    message_in, speeds, there, halo, freq, damping, coupling, message_out, u_re, u_im, omega_out, c_high, c_low
):
    count = freq.shape[1]
    total = u_re.shape[0]
    tail = halo[halo.shape[0] - 16 :, :].astype(f32)
    tail = tail[0:1, : total // 2] * CODE + tail[0:1, total // 2 :]
    odd = jnp.concatenate([speeds[...].astype(f32), tail], 1)
    even = jnp.concatenate([there[2:3, :], there[3:4, :]], 1)
    index = jnp.where(odd_core() == 0, even, odd)
    message_out[...] = message_in[...]
    omega = 0.25 + 4.0 * index / NGRID
    omega = jnp.transpose(jnp.broadcast_to(omega, (8, total)))[:, 0:1]
    omega = jnp.broadcast_to(omega, (total, count))
    f = freq[...]
    zeta = damping[...]
    d_re = f * f - omega * omega
    d_im = 2.0 * (zeta * f) * omega
    scale = omega / (d_re * d_re + d_im * d_im)
    u_re[...] = d_re * scale
    u_im[...] = d_im * scale
    omega_out[...] = omega[:, :128]
    i = lax.broadcasted_iota(jnp.int32, (count, count), 0)
    j = lax.broadcasted_iota(jnp.int32, (count, count), 1)
    coupled = jnp.transpose(coupling[...]) * (zeta * f * (1.5 / math.sqrt(count)))
    c_high[...], c_low[...] = split(jnp.where(i == j, 0.0, coupled))


def prepare(message, speeds, there, halo, freq, damping, coupling):
    total, count = 2 * speeds.shape[1], freq.shape[0]
    operands = (message, speeds, there, halo, freq.reshape(1, count), damping.reshape(1, count), coupling)
    return call(
        prepare_body,
        [
            sds(message.shape, f32),
            sds((total, count), f32),
            sds((total, count), f32),
            sds((total, 128), f32),
            sds((count, count), bf16),
            sds((count, count), bf16),
        ],
        operands,
        specs=[VMEM] * 7,
        microseconds=0.9,
    )


def solve_body(mine, other, u_re, u_im, omega, c_high, c_low, for_re, for_im):
    force = jnp.where(odd_core() == 1, mine[...], other[...])
    f_re, f_im = force[0:1, :], force[1:2, :]
    ch, cl = c_high[...], c_low[...]

    def coupled(y, sweep):
        if sweep < EARLY:
            return mm(y.astype(bf16), ch)
        high, low = split(y)
        return mm(high, ch) + (mm(low, ch) + mm(high, cl))

    total, count = u_re.shape
    tile = 256
    tiles = [pl.ds(t, tile) for t in range(0, total, tile)]
    state = []
    for s in tiles:
        ur, ui = u_re[s, :], u_im[s, :]
        state.append((f_re * ur + f_im * ui, f_im * ur - f_re * ui))
    for sweep in range(ITERS):
        after = []
        for s, (yr, yi) in zip(tiles, state):
            pr, pi = coupled(yr, sweep), coupled(yi, sweep)
            ur, ui = u_re[s, :], u_im[s, :]
            top_re, top_im = f_re + pi, f_im - pr
            after.append((top_re * ur + top_im * ui, top_im * ur - top_re * ui))
        state = after
    for s, (yr, yi) in zip(tiles, state):
        w = jnp.concatenate([omega[s, :]] * (count // 128), 1)
        re, im = (yr * w).astype(bf16), (yi * w).astype(bf16)
        for_re[s, :count] = re
        for_re[s, count:] = -im
        for_im[s, :count] = im
        for_im[s, count:] = re


def solve(mine, other, prepared):
    total, count = prepared[0].shape
    operands = (mine, other, *prepared)
    shape = sds((total, 2 * count), bf16)
    return call(solve_body, [shape, shape], operands, specs=[VMEM] * 7, microseconds=4.0)


def peaks_tile(modes, for_re, for_im):
    total = for_im.shape[0]
    tile = 256
    best = jnp.zeros((8, modes.shape[1]), f32)
    for s in range(0, total, tile):
        re = mm(for_re[s : s + tile, :], modes)
        im = mm(for_im[s : s + tile, :], modes)
        square = re * re + im * im
        best = jnp.maximum(best, jnp.max(square.reshape(tile // 8, 8, modes.shape[1]), axis=0))
    return best


def parts_of(parts):
    at = 0
    for part in parts:
        for e in range(0, part.shape[1], BLOCK):
            yield at, part, e
            at += BLOCK


def half_peaks_body(for_re, for_im, far, middle, near, best):
    for at, part, e in parts_of((far, middle, near)):
        best[:, at : at + BLOCK] = peaks_tile(part[:, e : e + BLOCK], for_re, for_im)


def all_peaks_body(for_im, before, far, middle, near, out, for_re):
    count = for_im.shape[1] // 2
    for_re[:, :count] = for_im[:, count:]
    for_re[:, count:] = -for_im[:, :count]
    rows = out.shape[1]
    even = odd_core() == 0
    for at, part, e in parts_of((far, middle, near)):
        best = jnp.maximum(before[:, at : at + BLOCK], peaks_tile(part[:, e : e + BLOCK], for_re, for_im))
        peak = jnp.sqrt(jnp.max(best, axis=0, keepdims=True))
        first, last = e, rows - 2 * BLOCK + e
        if part is middle:
            to = 2 * BLOCK + e
        elif part is near:
            to = jnp.where(even, last, first)
        elif e < 2 * BLOCK:
            to = jnp.where(even, first, last)
        else:
            to = 5 * BLOCK
        out[0:1, pl.ds(pl.multiple_of(to, BLOCK), BLOCK)] = peak


def peaks(for_re, for_im, parts):
    total, twice = for_im.shape
    rows = sum(p.shape[1] for p in parts)
    there = lax.ppermute(for_im, "slab", CORE_PAIRS)
    best = call(half_peaks_body, [sds((8, rows), f32)], (for_re, for_im, *parts), microseconds=2.5)[0]
    out = call(
        all_peaks_body,
        [sds((1, rows), f32)],
        (there, best, *parts),
        [pltpu.VMEM((total, twice), bf16)],
        [VMEM] * 5,
        2.5,
    )[0]
    return out.reshape(rows)


def on_device(
    mode_shapes,
    unbalance,
    connectivity,
    stress_weights,
    face_low_nodes,
    face_high_nodes,
    natural_freq,
    damping_ratio,
    coupling,
    speed_index,
):
    rows, width = mode_shapes.shape
    reach = face_low_nodes.shape[0]
    low = face_low_nodes.reshape(1, reach)
    high = face_high_nodes.reshape(1, reach)

    speeds = speed_index.reshape(1, -1)
    shapes = call(
        load_body,
        [sds((rows, width), bf16)],
        (mode_shapes,),
        [pltpu.SemaphoreType.DMA((4,))],
        [HBM],
        1.5,
        ROOM0,
    )[0]
    force = call(force_body, [sds((2, width // 2), f32)], (unbalance, shapes), microseconds=0.5)[0]
    small = sds((2, width // 2), f32)
    letter = sds((4, width // 2), f32)
    tables = pltpu.VMEM((2, WINDOW, BLOCK), bf16)
    table = pltpu.VMEM((rows, reach), bf16)

    def swap(x, number):
        return lax.ppermute(x, ("slab", "spd"), ROUNDS[number])

    def middle(blocks, force):
        return call(
            functools.partial(middle_body, blocks=blocks),
            [sds(force.shape, f32), sds((width, len(blocks) * BLOCK), bf16)],
            (force, connectivity, stress_weights, shapes_t),
            [tables],
            microseconds=MICRO * 2.2,
        )

    def end(halo, low_core, inner, force):
        return call(
            functools.partial(end_body, low_core=low_core, inner=inner),
            [small, sds((width, (2 + len(inner)) * BLOCK), bf16)],
            (force, connectivity, stress_weights, shapes_t, halo),
            [pltpu.VMEM((width, 3 * reach), bf16), tables],
            [VMEM] * 5,
            MICRO * 1.6,
        )

    arrived = lax.ppermute(force, "slab", CORE_PAIRS)
    force, shapes_t = call(
        turn_body, [small, sds((width, rows), bf16)], (force, shapes), microseconds=MICRO * 0.6
    )
    own = speeds.astype(f32)
    message = jnp.concatenate([force + arrived, own, own])
    arrived = swap(message, 0)
    message, far_rows = call(
        far_gather_body,
        [letter, sds((width, reach), bf16)],
        (message, low, high, shapes_t),
        [table],
        [VMEM] * 4,
        MICRO * 1.8,
    )
    far_halo = lax.ppermute(far_rows, ("slab", "spd"), FAR_PAIRS)
    message = jnp.concatenate([message[:2] + arrived[:2], message[2:3], arrived[2:3]])
    there = swap(message, 1)
    message, central = middle((2, 3, 4), message)
    force = message[:2] + there[:2]
    arrived, neighbour = swap(force, 2), arrived[2:3]
    force, near_rows = call(
        near_gather_body,
        [small, sds((width + 16, reach), bf16)],
        (force, neighbour, low, high, shapes_t),
        [table],
        [VMEM] * 5,
        MICRO * 1.8,
    )
    near_halo = lax.ppermute(near_rows, "slab", CORE_PAIRS)
    force = force + arrived
    arrived = swap(force, 3)
    force, far = end(far_halo, 0, (5,), force)
    force = force + arrived
    arrived = swap(force, 4)
    force, near = end(near_halo, 1, (), force)
    force, *prepared = prepare(force, speeds, there, near_halo, natural_freq, damping_ratio, coupling)
    force = force + arrived
    for_re, for_im = solve(force, lax.ppermute(force, "slab", CORE_PAIRS), prepared)
    return peaks(for_re, for_im, (far, central, near))


def solution(mesh):
    return jax.shard_map(
        on_device,
        mesh=mesh,
        in_specs=(
            P("slab", None),
            P(None, "slab"),
            P(None, "slab"),
            P(None, "slab"),
            P("slab"),
            P("slab"),
            P(),
            P(),
            P(),
            P("spd"),
        ),
        out_specs=P("slab"),
        check_vma=False,
    )
```

```python
import functools
import math

import jax
import jax.numpy as jnp
from jax import lax
from jax.experimental import pallas as pl
from jax.experimental.pallas import tpu as pltpu
from jax.sharding import PartitionSpec as P

ITERS = 6
EARLY = 5
NGRID = 4096
X, Y, Z, CORES = 4, 4, 8, 2
BLOCK = 256
WINDOW = 1280
CODE = 64
ROOM0 = 51
MICRO = 8.0
bf16 = jnp.bfloat16
f32 = jnp.float32


def mm(a, b):
    return jnp.dot(a, b, preferred_element_type=f32)


VMEM = pl.BlockSpec(memory_space=pltpu.VMEM)
HBM = pl.BlockSpec(memory_space=pltpu.HBM)


def call(body, out_shape, operands, scratch=(), specs=None, microseconds=1.0, room=24):
    return pl.pallas_call(
        body,
        out_shape=out_shape,
        in_specs=specs or [VMEM] * len(operands),
        out_specs=[VMEM] * len(out_shape),
        scratch_shapes=list(scratch),
        compiler_params=pltpu.CompilerParams(vmem_limit_bytes=int(room * 2**20)),
        cost_estimate=pl.CostEstimate(flops=int(1e9 * microseconds), bytes_accessed=0, transcendentals=0),
    )(*operands)


def sds(shape, dtype):
    return jax.ShapeDtypeStruct(shape, dtype)


def odd_core():
    return lax.rem(lax.axis_index("slab"), CORES)


def end_slab():
    slab = lax.axis_index("slab")
    return jnp.logical_or(slab == 0, slab == N_SLAB - 1)


def slab_of(x, z, c):
    return (x * Z + z) * CORES + c


def slab_pairs(partner):
    return [
        (slab_of(x, z, c), slab_of(*partner(x, z, c)))
        for x in range(X)
        for z in range(Z)
        for c in range(CORES)
    ]


CORE_PAIRS = slab_pairs(lambda x, z, c: (x, z, 1 - c))


def near_row(x, z, y):
    return y ^ 1


def mirror_row(x, z, y):
    return Y - 1 - y


def patient(x, z):
    return z == 0 and x > 0


def odd_round(partner, row=near_row):
    pairs = []
    for x in range(X):
        for z in range(Z):
            for y in range(Y):
                pairs.append((slab_of(x, z, 0) * Y + y, slab_of(x, z, 0) * Y + row(x, z, y)))
                pairs.append((slab_of(x, z, 1) * Y + y, slab_of(*partner(x, z), 1) * Y + y))
    return sorted(pairs)


ROUNDS = (
    odd_round(lambda x, z: (x ^ 1, z), lambda x, z, y: (mirror_row if patient(x, z) else near_row)(x, z, y)),
    odd_round(lambda x, z: (3 - x, z), lambda x, z, y: (near_row if patient(x, z) else mirror_row)(x, z, y)),
    odd_round(lambda x, z: (x, z ^ 1)),
    odd_round(lambda x, z: (x, z ^ 2)),
    odd_round(lambda x, z: (x, 7 - z)),
)
N_SLAB = X * Z * CORES
FAR_PAIRS = [
    (j * Y + y, (j + 1 if j % 2 else j - 1) * Y + y) if 0 < j < N_SLAB - 1 else (j * Y + y, j * Y + (y ^ 1))
    for j in range(N_SLAB)
    for y in range(Y)
]


def load_body(shapes, landing, sems):
    parts = sems.shape[0]
    step = shapes.shape[0] // parts
    copies = []
    for p in range(parts):
        s = pl.ds(p * step, step)
        copy = pltpu.make_async_copy(shapes.at[s, :], landing.at[s, :], sems.at[p])
        copy.start()
        copies.append(copy)
    for copy in copies:
        copy.wait()


def force_body(unbalance, shapes, force):
    total = mm(unbalance[...], shapes[...])
    half = total.shape[1] // 2
    force[0:1, :] = total[0:1, :half] - total[1:2, half:]
    force[1:2, :] = total[0:1, half:] + total[1:2, :half]


def turn_body(force_in, shapes, force_out, shapes_t):
    rows = shapes.shape[0]
    for r in range(0, rows, 2 * BLOCK):
        shapes_t[:, r : r + 2 * BLOCK] = jnp.transpose(shapes[r : r + 2 * BLOCK, :])
    force_out[...] = force_in[...]


def gather_rows(nodes, one, shapes_t, table):
    rows = shapes_t.shape[1]
    count = nodes.shape[1]
    here = jnp.broadcast_to(nodes.astype(jnp.int16), (16, count))
    row = lax.broadcasted_iota(jnp.int16, (16, count), 0)
    zero = jnp.zeros((16, count), bf16)
    for r in range(0, rows, 16):
        table[r : r + 16, :] = jnp.where(here == row + jnp.int16(r), one, zero)
    return mm(shapes_t[...], table[...]).astype(bf16)


def near_gather_body(message_in, speeds, low, high, shapes_t, message_out, out, table):
    width = shapes_t.shape[0]
    nodes = jnp.where(odd_core() == 0, high[...], low[...])
    one = jnp.ones((16, nodes.shape[1]), bf16)
    out[:width, :] = gather_rows(nodes, one, shapes_t, table)
    index = speeds[...].astype(jnp.int32)
    coarse = index // CODE
    fine = index - coarse * CODE
    row = jnp.concatenate([coarse.astype(f32), fine.astype(f32)], 1)
    out[width:, :] = jnp.broadcast_to(row, (16, row.shape[1])).astype(bf16)
    message_out[...] = message_in[...]


def far_gather_body(message_in, low, high, shapes_t, message_out, out, table):
    nodes = jnp.where(odd_core() == 0, low[...], high[...])
    one = jnp.full((16, nodes.shape[1]), jnp.where(end_slab(), 0.0, 1.0), f32).astype(bf16)
    out[...] = gather_rows(nodes, one, shapes_t, table)
    message_out[...] = message_in[...]


def fill_table(table, links, weights, start):
    corners, count = links.shape
    here = (links - start).astype(jnp.int16)
    here = [jnp.broadcast_to(here[k : k + 1, :], (16, count)) for k in range(corners)]
    value = [jnp.broadcast_to(weights[k : k + 1, :], (16, count)) for k in range(corners)]
    row = lax.broadcasted_iota(jnp.int16, (16, count), 0)
    for r in range(0, WINDOW, 16):
        at = row + jnp.int16(r)
        entry = jnp.zeros((16, count), bf16)
        for k in range(corners):
            entry = jnp.where(here[k] == at, value[k], entry)
        table[r : r + 16, :] = entry


def middle_body(force_in, links, weights, shapes_t, force_out, out, tables, *, blocks):
    for i, b in enumerate(blocks):
        s = slice(b * BLOCK, (b + 1) * BLOCK)
        fill_table(tables.at[i % 2], links[:, s], weights[:, s], b * BLOCK)
        start = (b - 2) * BLOCK
        modes = mm(shapes_t[:, start : start + WINDOW], tables[i % 2])
        out[:, i * BLOCK : (i + 1) * BLOCK] = modes.astype(bf16)
    force_out[...] = force_in[...]


def end_body(force_in, links, weights, shapes_t, halo, force_out, out, window, tables, *, low_core, inner):
    width, rows = shapes_t.shape
    reach = halo.shape[1]
    own = 1024

    low = odd_core() == low_core

    @pl.when(low)
    def _():
        window[:, :reach] = halo[:width, :]
        window[:, reach:] = shapes_t[:, :own]

    @pl.when(jnp.logical_not(low))
    def _():
        window[:, :own] = shapes_t[:, rows - own :]
        window[:, own:] = halo[:width, :]

    base = jnp.where(low, 0, rows - 2 * BLOCK)
    for i in range(2):
        start = pl.multiple_of(base + i * BLOCK, BLOCK)
        fill_table(tables.at[i], links[:, pl.ds(start, BLOCK)], weights[:, pl.ds(start, BLOCK)], start)
        modes = mm(window[:, i * BLOCK : i * BLOCK + WINDOW], tables[i])
        out[:, i * BLOCK : (i + 1) * BLOCK] = modes.astype(bf16)
    for i, b in enumerate(inner):
        s = slice(b * BLOCK, (b + 1) * BLOCK)
        fill_table(tables.at[i % 2], links[:, s], weights[:, s], b * BLOCK)
        modes = mm(shapes_t[:, (b - 2) * BLOCK : (b - 2) * BLOCK + WINDOW], tables[i % 2])
        out[:, (2 + i) * BLOCK : (3 + i) * BLOCK] = modes.astype(bf16)
    force_out[...] = force_in[...]


def split(x):
    high = x.astype(bf16)
    return high, (x - high.astype(f32)).astype(bf16)


def prepare_body(
    message_in, speeds, there, halo, freq, damping, coupling, message_out, u_re, u_im, omega_out, c_high, c_low
):
    count = freq.shape[1]
    total = u_re.shape[0]
    tail = halo[halo.shape[0] - 16 :, :].astype(f32)
    tail = tail[0:1, : total // 2] * CODE + tail[0:1, total // 2 :]
    odd = jnp.concatenate([speeds[...].astype(f32), tail], 1)
    even = jnp.concatenate([there[2:3, :], there[3:4, :]], 1)
    index = jnp.where(odd_core() == 0, even, odd)
    message_out[...] = message_in[...]
    omega = 0.25 + 4.0 * index / NGRID
    omega = jnp.transpose(jnp.broadcast_to(omega, (8, total)))[:, 0:1]
    omega = jnp.broadcast_to(omega, (total, count))
    f = freq[...]
    zeta = damping[...]
    d_re = f * f - omega * omega
    d_im = 2.0 * (zeta * f) * omega
    scale = omega / (d_re * d_re + d_im * d_im)
    u_re[...] = d_re * scale
    u_im[...] = d_im * scale
    omega_out[...] = omega[:, :128]
    i = lax.broadcasted_iota(jnp.int32, (count, count), 0)
    j = lax.broadcasted_iota(jnp.int32, (count, count), 1)
    coupled = jnp.transpose(coupling[...]) * (zeta * f * (1.5 / math.sqrt(count)))
    c_high[...], c_low[...] = split(jnp.where(i == j, 0.0, coupled))


def prepare(message, speeds, there, halo, freq, damping, coupling):
    total, count = 2 * speeds.shape[1], freq.shape[0]
    operands = (message, speeds, there, halo, freq.reshape(1, count), damping.reshape(1, count), coupling)
    return call(
        prepare_body,
        [
            sds(message.shape, f32),
            sds((total, count), f32),
            sds((total, count), f32),
            sds((total, 128), f32),
            sds((count, count), bf16),
            sds((count, count), bf16),
        ],
        operands,
        specs=[VMEM] * 7,
        microseconds=0.9,
    )


def solve_body(mine, other, u_re, u_im, omega, c_high, c_low, for_re, for_im):
    force = jnp.where(odd_core() == 1, mine[...], other[...])
    f_re, f_im = force[0:1, :], force[1:2, :]
    ch, cl = c_high[...], c_low[...]

    def coupled(y, sweep):
        if sweep < EARLY:
            return mm(y.astype(bf16), ch)
        high, low = split(y)
        return mm(high, ch) + (mm(low, ch) + mm(high, cl))

    total, count = u_re.shape
    tile = 256
    tiles = [pl.ds(t, tile) for t in range(0, total, tile)]
    state = []
    for s in tiles:
        ur, ui = u_re[s, :], u_im[s, :]
        state.append((f_re * ur + f_im * ui, f_im * ur - f_re * ui))
    for sweep in range(ITERS):
        after = []
        for s, (yr, yi) in zip(tiles, state):
            pr, pi = coupled(yr, sweep), coupled(yi, sweep)
            ur, ui = u_re[s, :], u_im[s, :]
            top_re, top_im = f_re + pi, f_im - pr
            after.append((top_re * ur + top_im * ui, top_im * ur - top_re * ui))
        state = after
    for s, (yr, yi) in zip(tiles, state):
        w = jnp.concatenate([omega[s, :]] * (count // 128), 1)
        re, im = (yr * w).astype(bf16), (yi * w).astype(bf16)
        for_re[s, :count] = re
        for_re[s, count:] = -im
        for_im[s, :count] = im
        for_im[s, count:] = re


def solve(mine, other, prepared):
    total, count = prepared[0].shape
    operands = (mine, other, *prepared)
    shape = sds((total, 2 * count), bf16)
    return call(solve_body, [shape, shape], operands, specs=[VMEM] * 7, microseconds=4.0)


def peaks_tile(modes, for_re, for_im):
    total = for_im.shape[0]
    tile = 256
    best = jnp.zeros((8, modes.shape[1]), f32)
    for s in range(0, total, tile):
        re = mm(for_re[s : s + tile, :], modes)
        im = mm(for_im[s : s + tile, :], modes)
        square = re * re + im * im
        best = jnp.maximum(best, jnp.max(square.reshape(tile // 8, 8, modes.shape[1]), axis=0))
    return best


def parts_of(parts):
    at = 0
    for part in parts:
        for e in range(0, part.shape[1], BLOCK):
            yield at, part, e
            at += BLOCK


def half_peaks_body(for_re, for_im, far, middle, near, best):
    for at, part, e in parts_of((far, middle, near)):
        best[:, at : at + BLOCK] = peaks_tile(part[:, e : e + BLOCK], for_re, for_im)


def all_peaks_body(for_im, before, far, middle, near, out, for_re):
    count = for_im.shape[1] // 2
    for_re[:, :count] = for_im[:, count:]
    for_re[:, count:] = -for_im[:, :count]
    rows = out.shape[1]
    even = odd_core() == 0
    for at, part, e in parts_of((far, middle, near)):
        best = jnp.maximum(before[:, at : at + BLOCK], peaks_tile(part[:, e : e + BLOCK], for_re, for_im))
        peak = jnp.sqrt(jnp.max(best, axis=0, keepdims=True))
        first, last = e, rows - 2 * BLOCK + e
        if part is middle:
            to = 2 * BLOCK + e
        elif part is near:
            to = jnp.where(even, last, first)
        elif e < 2 * BLOCK:
            to = jnp.where(even, first, last)
        else:
            to = 5 * BLOCK
        out[0:1, pl.ds(pl.multiple_of(to, BLOCK), BLOCK)] = peak


def peaks(for_re, for_im, parts):
    total, twice = for_im.shape
    rows = sum(p.shape[1] for p in parts)
    there = lax.ppermute(for_im, "slab", CORE_PAIRS)
    best = call(half_peaks_body, [sds((8, rows), f32)], (for_re, for_im, *parts), microseconds=2.5)[0]
    out = call(
        all_peaks_body,
        [sds((1, rows), f32)],
        (there, best, *parts),
        [pltpu.VMEM((total, twice), bf16)],
        [VMEM] * 5,
        2.5,
    )[0]
    return out.reshape(rows)


def on_device(
    mode_shapes,
    unbalance,
    connectivity,
    stress_weights,
    face_low_nodes,
    face_high_nodes,
    natural_freq,
    damping_ratio,
    coupling,
    speed_index,
):
    rows, width = mode_shapes.shape
    reach = face_low_nodes.shape[0]
    low = face_low_nodes.reshape(1, reach)
    high = face_high_nodes.reshape(1, reach)

    speeds = speed_index.reshape(1, -1)
    shapes = call(
        load_body,
        [sds((rows, width), bf16)],
        (mode_shapes,),
        [pltpu.SemaphoreType.DMA((4,))],
        [HBM],
        1.5,
        ROOM0,
    )[0]
    force = call(force_body, [sds((2, width // 2), f32)], (unbalance, shapes), microseconds=0.5)[0]
    small = sds((2, width // 2), f32)
    letter = sds((4, width // 2), f32)
    tables = pltpu.VMEM((2, WINDOW, BLOCK), bf16)
    table = pltpu.VMEM((rows, reach), bf16)

    def swap(x, number):
        return lax.ppermute(x, ("slab", "spd"), ROUNDS[number])

    def middle(blocks, force):
        return call(
            functools.partial(middle_body, blocks=blocks),
            [sds(force.shape, f32), sds((width, len(blocks) * BLOCK), bf16)],
            (force, connectivity, stress_weights, shapes_t),
            [tables],
            microseconds=MICRO * 2.2,
        )

    def end(halo, low_core, inner, force):
        return call(
            functools.partial(end_body, low_core=low_core, inner=inner),
            [small, sds((width, (2 + len(inner)) * BLOCK), bf16)],
            (force, connectivity, stress_weights, shapes_t, halo),
            [pltpu.VMEM((width, 3 * reach), bf16), tables],
            [VMEM] * 5,
            MICRO * 1.6,
        )

    arrived = lax.ppermute(force, "slab", CORE_PAIRS)
    force, shapes_t = call(
        turn_body, [small, sds((width, rows), bf16)], (force, shapes), microseconds=MICRO * 0.6
    )
    own = speeds.astype(f32)
    message = jnp.concatenate([force + arrived, own, own])
    arrived = swap(message, 0)
    message, far_rows = call(
        far_gather_body,
        [letter, sds((width, reach), bf16)],
        (message, low, high, shapes_t),
        [table],
        [VMEM] * 4,
        MICRO * 1.8,
    )
    far_halo = lax.ppermute(far_rows, ("slab", "spd"), FAR_PAIRS)
    message = jnp.concatenate([message[:2] + arrived[:2], message[2:3], arrived[2:3]])
    there, neighbour = swap(message, 1), message[3:4]
    message, near_rows = call(
        near_gather_body,
        [letter, sds((width + 16, reach), bf16)],
        (message, neighbour, low, high, shapes_t),
        [table],
        [VMEM] * 5,
        MICRO * 1.8,
    )
    near_halo = lax.ppermute(near_rows, "slab", CORE_PAIRS)
    force = message[:2] + there[:2]
    arrived = swap(force, 2)
    force, central = middle((2, 3, 4), force)
    force = force + arrived
    arrived = swap(force, 3)
    force, far = end(far_halo, 0, (5,), force)
    force = force + arrived
    arrived = swap(force, 4)
    force, near = end(near_halo, 1, (), force)
    force, *prepared = prepare(force, speeds, there, near_halo, natural_freq, damping_ratio, coupling)
    force = force + arrived
    for_re, for_im = solve(force, lax.ppermute(force, "slab", CORE_PAIRS), prepared)
    return peaks(for_re, for_im, (far, central, near))


def solution(mesh):
    return jax.shard_map(
        on_device,
        mesh=mesh,
        in_specs=(
            P("slab", None),
            P(None, "slab"),
            P(None, "slab"),
            P(None, "slab"),
            P("slab"),
            P("slab"),
            P(),
            P(),
            P(),
            P("spd"),
        ),
        out_specs=P("slab"),
        check_vma=False,
    )
```
